128 devices in a mesh: dp: 16 (over x, y), ep: 8 (over z, core).
Axes of the slice: x: 4, y: 4, z: 4, core: 2. Of those that a mesh axis runs over, the one named last changes fastest.
Arguments:
- queries_c: bfloat16 [2048, 32768], P('dp', 'ep'), may hold values from -17 to 17
- queries_r: bfloat16 [2048, 4096], P('dp', 'ep'), may hold values from -17 to 17
- latents: bfloat16 [2048, 512], P('dp'), may hold values from -4 to 4
- key_rope: bfloat16 [64, 2048], P(None, 'dp'), may hold values from -4 to 4
- value_up: bfloat16 [64, 512, 128], P('ep'), may hold values from -0.25 to 0.25
- out_proj: bfloat16 [8192, 3584], P('ep'), may hold values from -0.0625 to 0.0625
- norm_gain: float32 [3584], replicated, may hold values from 0.1 to 1.9
- router: bfloat16 [3584, 16], replicated, may hold values from -0.09375 to 0.09375
- gate_up: bfloat16 [16, 2, 3584, 2048], P('dp', None, None, 'ep'), may hold values from -0.09375 to 0.09375
- down: bfloat16 [16, 2048, 3584], P('dp', 'ep'), may hold values from -0.125 to 0.125
- routes: int32 [2048, 2], P(('dp', 'ep')), may hold values from 0 to 15, all different within a row; in each aligned block of 16 rows (0 to 15, 16 to 31, ...) at most 2 rows name the same one
- lengths: int32 [16], replicated, may hold values from 32 to 128, as said below
- plan: int32 [16], replicated, may hold values from 0 to 15, as said below
Outputs:
- layer_out: bfloat16 [2048, 3584], P(('dp', 'ep'))
The draws below stay inside these ranges and needn't reach their ends.
Inputs may be any that keep to these rules, and one draw needn't show every extreme that they name: Prompt r fills positions 0 to lengths[r] - 1 of its buffer; some prompt fills all 128; half of the prompts reach into their last block and the other half are at most 64 long. A permutation of the ranks that pairs them: the last 16 positions of prompt r are processed on rank plan[r], plan[plan[r]] = r and plan[r] != r; the k-th shortest prompt is paired with the k-th longest (ties broken by rank). `routes`: each row names 2 different experts; within the rows of one device (16 aligned rows) no expert is named more than 2 times.
All inputs are finite; a program needn't handle non-finite values.
Results may differ from the reference program's by a relative error of at most 0.033.
Values may be sent and summed in bfloat16 or wider, within the bound.
A program may use at most 64 MiB of HBM per device.

```python
import math
import jax
import jax.numpy as jnp
import numpy as np
from jax import lax

D = 3584
LAT = 512
ROPE = 64
HEADS = 64
VDIM = 128
FF = 2048
ROUTES = 2
S = 128
SPAN = 16
ROWS_DEV = 16
EXPERTS = 16
CAP = 2
TOKENS = 2048
N_DP = 16
N_EP = 8


def latent_basis(key):
    gauss = jnp.clip(jax.random.normal(key, (TOKENS, LAT + ROPE), jnp.float32), -4.0, 4.0)
    return gauss


def prompt_plan(key):
    shuffled = jax.random.permutation(jax.random.fold_in(key, 2), N_DP).astype(jnp.int32)
    longer = shuffled < N_DP // 2
    long_sizes = jax.random.randint(key, (N_DP,), S - SPAN // 2, S + 1)
    short_sizes = jax.random.randint(jax.random.fold_in(key, 1), (N_DP,), S // 4, S // 2 + 1)
    sizes = jnp.where(longer, long_sizes, short_sizes)
    sizes = jnp.where(shuffled == 0, S, sizes).astype(jnp.int32)
    order = jnp.argsort(sizes * N_DP + jnp.arange(N_DP, dtype=jnp.int32), stable=True).astype(jnp.int32)
    helper_rank = jnp.zeros((N_DP,), jnp.int32).at[order].set(order[::-1])
    return (sizes, helper_rank)


def draw_latents(key, part):
    gauss = latent_basis(key)
    chosen = gauss
    return chosen[:, :LAT].astype(jnp.bfloat16)


def draw_key_rope(key, part):
    gauss = latent_basis(key)
    chosen = gauss
    return jnp.transpose(chosen[:, LAT:]).astype(jnp.bfloat16)


def draw_queries_c(key, part):
    key = jax.random.fold_in(key, 5)
    result = 0.6 * jnp.clip(jax.random.normal(key, (TOKENS, HEADS, LAT), jnp.float32), -4.0, 4.0)
    return result.reshape(TOKENS, HEADS * LAT).astype(jnp.bfloat16)


def draw_queries_r(key, part):
    key = jax.random.fold_in(key, 6)
    result = 0.6 * jnp.clip(jax.random.normal(key, (TOKENS, HEADS, ROPE), jnp.float32), -4.0, 4.0)
    return result.reshape(TOKENS, HEADS * ROPE).astype(jnp.bfloat16)


def draw_lengths(key, part):
    sizes, helper_rank = prompt_plan(key)
    return sizes


def draw_plan(key, part):
    sizes, helper_rank = prompt_plan(key)
    return helper_rank


def shard_levels(stream_key, shape, cuts, smallest, largest):
    factor_of = 1.0
    for axis_at, shards_of in cuts:
        heights = jax.random.uniform(jax.random.fold_in(jax.random.fold_in(stream_key, 6), axis_at), (shards_of,), jnp.float32, smallest / len(cuts), largest / len(cuts))
        factor_of = factor_of * jnp.repeat(jnp.exp(heights), shape[axis_at] // shards_of).reshape((-1,) + (1,) * (len(shape) - 1 - axis_at))
    return factor_of


def assign_block(key, own, number, rows, amount, top, most, slope):
    ranking = jax.random.permutation(key, amount)
    crowded, usual = portions_of(amount, rows * top, most, slope, True), portions_of(amount, rows * top, most, slope, False)
    places = jnp.arange(amount)

    def named(tallies, rotation):
        used = int((tallies > 0).sum())
        fixed = max(1, used // 4)
        passed = fixed + (places - fixed + rotation * (used - fixed)) % max(1, amount - fixed)
        return jnp.zeros((amount,), jnp.int32).at[ranking[jnp.where(places < fixed, places, passed)]].set(jnp.asarray(tallies, jnp.int32))

    tallies = jnp.where(number % 4 == 0, named(crowded, number // 4), named(usual, number - number // 4 - 1))
    mixed = jax.random.permutation(jax.random.fold_in(own, 3), amount)
    donor, taker = mixed[0:amount // 2 * 2:2], mixed[1:amount // 2 * 2:2]
    margin = jnp.minimum(tallies[donor] - 1, most - tallies[taker]) // 2
    margin = jnp.where((donor == ranking[0]) | (taker == ranking[0]) | (tallies[taker] == 0), 0, jnp.maximum(margin, 0))
    passed = jax.random.randint(jax.random.fold_in(own, 4), (amount // 2,), 0, 1 << 20) % (margin + 1)
    tallies = tallies.at[donor].add(-passed).at[taker].add(passed)
    labels = jnp.searchsorted(jnp.cumsum(tallies), jnp.arange(rows * top), side="right").astype(jnp.int32)
    listing = labels.reshape(top, rows).T
    listing = listing[jax.random.permutation(jax.random.fold_in(own, 1), rows)]
    rotation = jax.random.randint(jax.random.fold_in(own, 2), (rows, 1), 0, top)
    return jnp.take_along_axis(listing, (jnp.arange(top)[None, :] + rotation) % top, axis=1)


def portions_of(number_of, total, limit, lean, full):
    portions = [(1 << 20) // math.isqrt(standing ** lean) + 1 for standing in range(1, number_of + 1)]
    largest = limit if full else min(limit, max(-(-total // number_of), total * portions[0] // sum(portions)))
    least = 1 if total - largest >= number_of - 1 else 0
    holding, rest = [largest] + [least] * (number_of - 1), total - largest - least * (number_of - 1)
    while rest > 0:
        candidates = [i for i in range(1, number_of) if holding[i] < largest] or [i for i in range(1, number_of) if holding[i] < limit]
        mass, remaining = sum([portions[i] for i in candidates]), rest
        for i in candidates:
            more = min(limit - holding[i], max(1, remaining * portions[i] // mass), rest)
            holding[i] = holding[i] + more
            rest = rest - more
    return np.array(holding)


def scatter_about(key, shape, scale, most, cuts=(), kind=jnp.bfloat16):
    factor_of = shard_levels(key, shape, cuts, -0.22, 0.18) if cuts else 1.0
    array = jax.random.normal(key, shape, jnp.float32) * scale * factor_of
    return jnp.minimum(jnp.maximum(array, -most), most).astype(kind)


def setup_inputs(seed: int = 0) -> dict:
    streams_of = jax.random.split(jax.random.key(seed), 14)
    queries_c = draw_queries_c(jax.random.fold_in(streams_of[13], 71), 0)
    queries_r = draw_queries_r(jax.random.fold_in(streams_of[13], 71), 0)
    latents = draw_latents(jax.random.fold_in(streams_of[13], 71), 0)
    key_rope = draw_key_rope(jax.random.fold_in(streams_of[13], 71), 0)
    value_up = scatter_about(streams_of[4], (HEADS, LAT, VDIM), LAT ** -0.5, 0.25, ((0, 8),))
    out_proj = scatter_about(streams_of[5], (HEADS * VDIM, D), (HEADS * VDIM) ** -0.5, 0.0625, ((0, 8),))
    norm_gain = jnp.clip(1.0 + 0.18 * jax.random.normal(streams_of[6], (D,), jnp.float32), 0.1, 1.9)
    router = scatter_about(streams_of[7], (D, EXPERTS), D ** -0.5, 0.09375)
    gate_up = scatter_about(streams_of[8], (EXPERTS, 2, D, FF), D ** -0.5, 0.09375, ((0, 16), (3, 8)))
    down = scatter_about(streams_of[9], (EXPERTS, FF, D), FF ** -0.5, 0.125, ((0, 16), (1, 8)))
    routes_keys = jax.random.split(jax.random.fold_in(streams_of[10], 1), TOKENS // ROWS_DEV)
    routes_turns = jax.random.permutation(jax.random.fold_in(streams_of[10], 3), TOKENS // ROWS_DEV)
    routes = jax.vmap(lambda own, number: assign_block(jax.random.fold_in(streams_of[10], 2), own, number, ROWS_DEV, EXPERTS, ROUTES, CAP, 2))(routes_keys, routes_turns).reshape((TOKENS, ROUTES))
    lengths = draw_lengths(jax.random.fold_in(streams_of[13], 71), 0)
    plan = draw_plan(jax.random.fold_in(streams_of[13], 71), 0)
    return dict(queries_c=queries_c, queries_r=queries_r, latents=latents, key_rope=key_rope, value_up=value_up, out_proj=out_proj, norm_gain=norm_gain, router=router, gate_up=gate_up, down=down, routes=routes, lengths=lengths, plan=plan)


softmax_scale = 192.0 ** (-0.5)
route_scale = 2.5
norm_eps = 1e-06

def attend(queries, rotary, latent_rows, key_rotary, positions, length):
    wide = jnp.float32
    scores = jnp.einsum('ihc,jc->hij', queries.astype(wide), latent_rows.astype(wide))
    scores = (scores + jnp.einsum('ihd,dj->hij', rotary.astype(wide), key_rotary.astype(wide))) * softmax_scale
    places = jnp.arange(latent_rows.shape[0], dtype=jnp.int32)
    visible = (places[None, :] <= positions[:, None]) & (places[None, :] < length)
    highest = lax.optimization_barrier(jnp.max(jnp.where(visible[None], scores, -jnp.inf), axis=2, keepdims=True))
    weights = jnp.where(visible[None], jnp.exp(scores - highest), 0.0)
    totals = lax.optimization_barrier(jnp.sum(weights, axis=2))
    probabilities = weights.astype(jnp.bfloat16)
    mixed = jnp.einsum('hij,jc->ihc', probabilities.astype(wide), latent_rows.astype(wide))
    mixed = mixed / jnp.transpose(totals)[:, :, None]
    return jnp.where((positions < length)[:, None, None], mixed, 0.0).astype(jnp.bfloat16)

def pair_slots(route_rows, experts, capacity):
    flat = route_rows.reshape(-1)
    onehot = (flat[:, None] == jnp.arange(experts, dtype=jnp.int32)[None, :]).astype(jnp.int32)
    before = jnp.cumsum(onehot, axis=0) - onehot
    position = lax.optimization_barrier(jnp.sum(before * onehot, axis=1))
    return (flat * capacity + position).astype(jnp.int32)

def place_matrix(slots, experts, capacity, rows, fanout):
    target = jnp.arange(experts * capacity, dtype=jnp.int32)
    return jnp.any(slots.reshape(rows, fanout)[None, :, :] == target[:, None, None], axis=2)

def reference(queries_c, queries_r, latents, key_rope, value_up, out_proj, norm_gain, router, gate_up, down, routes, lengths, plan):
    wide = jnp.float32
    prompt_q = queries_c.reshape(N_DP, S, HEADS, LAT)
    prompt_r = queries_r.reshape(N_DP, S, HEADS, ROPE)
    prompt_lat = latents.reshape(N_DP, S, LAT)
    prompt_key = jnp.transpose(key_rope.reshape(ROPE, N_DP, S), (1, 0, 2))
    positions = jnp.arange(S, dtype=jnp.int32)

    def one_prompt(pieces):
        return attend(pieces[0], pieces[1], pieces[2], pieces[3], positions, pieces[4])
    attended = lax.map(one_prompt, (prompt_q, prompt_r, prompt_lat, prompt_key, lengths))
    source = jnp.zeros((N_DP,), jnp.int32).at[plan].set(jnp.arange(N_DP, dtype=jnp.int32))
    placed = jnp.concatenate([attended[:, :S - SPAN], attended[source][:, S - SPAN:]], axis=1)
    placed = placed.reshape(TOKENS, HEADS, LAT)
    values = jnp.einsum('thc,hcv->thv', placed.astype(wide), value_up.astype(wide)).astype(jnp.bfloat16)
    values = values.reshape(TOKENS, HEADS * VDIM)
    mixed = jnp.dot(values, out_proj, preferred_element_type=wide)
    normed = (mixed * lax.rsqrt(lax.optimization_barrier(jnp.mean(mixed * mixed, axis=1, keepdims=True)) + norm_eps) * norm_gain).astype(jnp.bfloat16)
    logits = jnp.dot(normed, router, preferred_element_type=wide)
    chosen = jax.nn.sigmoid(jnp.take_along_axis(logits, routes, axis=1))
    route_weights = route_scale * chosen / lax.optimization_barrier(jnp.sum(chosen, axis=1, keepdims=True))
    blocks = TOKENS // ROWS_DEV
    block_routes = routes.reshape(blocks, ROWS_DEV, ROUTES)

    def block_slots(routed):
        return pair_slots(routed, EXPERTS, CAP)

    def block_places(chosen_slots):
        return place_matrix(chosen_slots, EXPERTS, CAP, ROWS_DEV, ROUTES)
    slots = jax.vmap(block_slots)(block_routes)
    places = jax.vmap(block_places)(slots).astype(wide)
    buffers = jnp.einsum('bsr,brd->bsd', places, normed.reshape(blocks, ROWS_DEV, D).astype(wide))
    per_expert = jnp.transpose(buffers.reshape(blocks, EXPERTS, CAP, D), (1, 0, 2, 3))
    per_expert = per_expert.reshape(EXPERTS, blocks * CAP, D).astype(jnp.bfloat16)

    def expert_slices(pieces):
        rows_in = pieces[0].astype(wide)
        gate = jnp.einsum('nd,dsf->nsf', rows_in, pieces[1][0].reshape(D, N_EP, FF // N_EP).astype(wide))
        upper = jnp.einsum('nd,dsf->nsf', rows_in, pieces[1][1].reshape(D, N_EP, FF // N_EP).astype(wide))
        hidden = (jax.nn.silu(gate) * upper).astype(jnp.bfloat16)
        parts = jnp.einsum('nsf,sfd->nsd', hidden.astype(wide), pieces[2].reshape(N_EP, FF // N_EP, D).astype(wide))
        return lax.optimization_barrier(jnp.sum(parts.astype(jnp.bfloat16).astype(wide), axis=1))
    outputs = lax.map(expert_slices, (per_expert, gate_up, down))
    by_block = jnp.transpose(outputs.reshape(EXPERTS, blocks, CAP, D), (1, 0, 2, 3)).reshape(blocks, EXPERTS * CAP, D)

    def pick_rows(table, chosen_slots):
        return jnp.take(table, chosen_slots, axis=0)
    pair_out = jax.vmap(pick_rows)(by_block, slots).reshape(TOKENS, ROUTES, D)
    return (mixed + lax.optimization_barrier(jnp.sum(route_weights[:, :, None] * pair_out, axis=1))).astype(jnp.bfloat16)
```

```python
import jax
import jax.numpy as jnp
from jax import lax
from jax.experimental import pallas as pl
from jax.experimental.pallas import tpu as pltpu
from jax.sharding import PartitionSpec as P

MESH = pl.DeviceIdType.MESH
BF = jnp.bfloat16
F32 = jnp.float32

D = 3584
LAT = 512
ROPE = 64
VDIM = 128
S = 128
SPAN = 16
HEADS_HERE = 8
N_DP = 16
N_Z = 4
HALF = 64
COLS = D // N_Z
SLOTS = 8
EXTRA = 128

softmax_scale = 192.0 ** (-0.5)
route_scale = 2.5
norm_eps = 1e-06


def mm(a, b):
    return jnp.dot(a, b, preferred_element_type=F32)


def attend(q, qr, lat, kr, position, length):
    scores = lax.dot_general(q, lat, (((1,), (1,)), ((), ())), preferred_element_type=F32)
    scores = (scores + mm(qr, kr)) * softmax_scale
    key = lax.broadcasted_iota(jnp.int32, scores.shape, 1)
    visible = (key <= position) & (key < length)
    highest = jnp.max(jnp.where(visible, scores, -jnp.inf), axis=1, keepdims=True)
    weights = jnp.where(visible, jnp.exp(scores - highest), 0.0)
    totals = jnp.sum(weights, axis=1, keepdims=True)
    mixed = mm(weights.astype(BF), lat) / totals
    return jnp.where(position[:, :1] < length, mixed, 0.0).astype(BF)


def kernel(
    lengths_s, plan_s,
    qc_h, qr_h, lat_h, kr_h, vu_h, op_h, gain_h, router_h, gu_h, dn_h, routes_h,
    out,
    qc, qr, lat, kr, vu, op, gain, router, gu, dn, rt,
    vals, mv, own, px_send, px_recv, rs_send, rs_recv, mixed,
    a_send, x, gate, upper, logit, square, hid,
    o_own, ox_send, ox_recv, os_send, os_recv, b_send, b_recv, f_send, f_recv,
    l_sem, q_sem, rt_s, rt_r, mv_s, mv_r, px_s, px_r, rs_s, rs_r, a_s, a_r, g_s, g_r, h_s, h_r,
    ox_s, ox_r, os_s, os_r, b_s, b_r, f_s, f_r,
):
    r = lax.axis_index("dp")
    ep = lax.axis_index("ep")
    z = ep // 2
    c = ep % 2
    sib = z * 2 + 1 - c

    def remote(src, dst, ssem, rsem, dp_to, ep_to):
        return pltpu.make_async_remote_copy(
            src_ref=src, dst_ref=dst, send_sem=ssem, recv_sem=rsem,
            device_id=(dp_to, ep_to), device_id_type=MESH)

    loads = [
        (lat_h, lat), (kr_h, kr), (vu_h, vu), (op_h, op), (routes_h, rt.at[z]),
        (gain_h, gain), (router_h, router), (gu_h.at[0], gu), (dn_h.at[0], dn),
    ]
    load = [pltpu.make_async_copy(s, d, l_sem.at[i]) for i, (s, d) in enumerate(loads)]
    qload = []
    for b in range(8):
        to = (b % 2) * HALF + (b // 2) * SPAN
        qload.append(pltpu.make_async_copy(
            qc_h.at[pl.ds(b * SPAN, SPAN)], qc.at[pl.ds(to, SPAN)], q_sem.at[b]))
        qload.append(pltpu.make_async_copy(
            qr_h.at[pl.ds(b * SPAN, SPAN)], qr.at[pl.ds(to, SPAN)], q_sem.at[8 + b]))
    load[0].start()
    load[1].start()
    for cp in reversed(qload):
        cp.start()
    for i in (2, 4, 3, 5, 6, 7, 8):
        load[i].start()

    barrier = pltpu.get_barrier_semaphore()

    def greet(i, carry):
        pl.semaphore_signal(barrier, inc=1, device_id=(lax.rem(r + i, N_DP), ep), device_id_type=MESH)
        return carry

    lax.fori_loop(1, N_DP, greet, 0)
    pl.semaphore_signal(barrier, inc=1, device_id=(r, sib), device_id_type=MESH)
    for dz in (1, 2, 3):
        pl.semaphore_signal(
            barrier, inc=1, device_id=(r, lax.rem(z + dz, N_Z) * 2 + c), device_id_type=MESH)
    pl.semaphore_wait(barrier, N_DP - 1 + 1 + 3)

    load[4].wait()
    for dz in (1, 2, 3):
        remote(rt.at[z], rt.at[z], rt_s.at[dz], rt_r.at[z], r, lax.rem(z + dz, N_Z) * 2 + c).start()

    length = lengths_s[r]
    load[0].wait()
    load[1].wait()
    qload[14].wait()
    qload[15].wait()
    latv = lat[...]
    krv = kr[...]
    q_last = jnp.concatenate(
        [qc[S - SPAN:, h * LAT:(h + 1) * LAT] for h in range(HEADS_HERE)], axis=0)
    r_last = jnp.concatenate(
        [qr[S - SPAN:, h * ROPE:(h + 1) * ROPE] for h in range(HEADS_HERE)], axis=0)
    place = lax.broadcasted_iota(jnp.int32, (HEADS_HERE * SPAN, S), 0)
    att = attend(q_last, r_last, latv, krv, S - SPAN + place % SPAN, length)
    load[2].wait()
    for h in range(HEADS_HERE):
        mv[r, :, h * VDIM:(h + 1) * VDIM] = mm(att[h * SPAN:(h + 1) * SPAN], vu[h]).astype(BF)

    def mv_copy(i):
        to = lax.rem(r + i, N_DP)
        return remote(mv.at[r], mv.at[r], mv_s.at[i], mv_r.at[r], to, ep)

    def mv_start(i, carry):
        mv_copy(i).start()
        return carry

    lax.fori_loop(1, N_DP, mv_start, 0)

    for i in range(14):
        qload[i].wait()
    rows = S - SPAN
    place = lax.broadcasted_iota(jnp.int32, (rows, S), 0)
    position = ((place % HALF) // SPAN * 2 + place // HALF) * SPAN + place % SPAN
    for h in range(HEADS_HERE):
        att = attend(
            qc[:rows, h * LAT:(h + 1) * LAT], qr[:rows, h * ROPE:(h + 1) * ROPE],
            latv, krv, position, length)
        vals[:rows, h * VDIM:(h + 1) * VDIM] = mm(att, vu[h]).astype(BF)

    for dz in (1, 2, 3):
        zz = lax.rem(z + dz, N_Z)
        remote(rt.at[zz], rt.at[zz], rt_s.at[dz], rt_r.at[zz], r, zz * 2 + c).wait_recv()
    first = jnp.concatenate([rt[i, 0:1, :] for i in range(N_Z)], axis=1)
    second = jnp.concatenate([rt[i, 1:2, :] for i in range(N_Z)], axis=1)
    slot = lax.broadcasted_iota(jnp.int32, (N_DP * SLOTS, HALF), 0)
    row = lax.broadcasted_iota(jnp.int32, (N_DP * SLOTS, HALF), 1)
    expert = slot // SLOTS
    named = jnp.where((first == expert) | (second == expert), 1.0, 0.0)
    t_row = lax.broadcasted_iota(jnp.int32, (HALF, HALF), 0)
    t_col = lax.broadcasted_iota(jnp.int32, (HALF, HALF), 1)
    earlier = jnp.where((t_row // SPAN == t_col // SPAN) & (t_row < t_col), 1.0, 0.0).astype(BF)
    before = mm(named.astype(BF), earlier)
    same = (slot // 2) % N_Z == row // SPAN
    chosen_slot = jnp.where(same & (before == (slot % 2).astype(F32)), named, 0.0)
    slots_t = chosen_slot.astype(BF)
    slots = chosen_slot.T.astype(BF)

    def mv_wait(i, carry):
        frm = lax.rem(r + i, N_DP)
        remote(mv.at[frm], mv.at[frm], mv_s.at[i], mv_r.at[frm], frm, ep).wait_recv()
        return carry

    lax.fori_loop(1, N_DP, mv_wait, 0)
    vals[rows:, :] = mv[plan_s[r]]

    load[3].wait()
    order = (2, 1, 3, 0)

    def px_copy(zz):
        return remote(px_send.at[zz], px_recv.at[zz], px_s.at[zz], px_r.at[zz], r, sib)

    def rs_copy(dz, zz):
        return remote(rs_send.at[zz], rs_recv.at[z], rs_s.at[dz], rs_r.at[z], r, zz * 2 + c)

    def pair_sum(dz):
        zz = lax.rem(z + dz, N_Z)
        px_copy(zz).wait_recv()
        total = own[zz] + px_recv[zz].astype(F32)
        if dz:
            rs_send[zz] = total.astype(BF)
            rs_copy(dz, zz).start()
        else:
            mixed[...] = total

    valv = vals[...]
    for n, dz in enumerate(order):
        zz = lax.rem(z + dz, N_Z)
        block = mm(valv, op[:, pl.ds(pl.multiple_of(zz * COLS, 128), COLS)])
        top, bottom = block[:HALF], block[HALF:]
        own[zz] = jnp.where(c == 0, top, bottom)
        px_send[zz] = jnp.where(c == 0, bottom, top).astype(BF)
        px_copy(zz).start()
        if n:
            pair_sum(order[n - 1])
    pair_sum(order[-1])
    total = mixed[...]
    for dz in (1, 3, 2):
        zz = lax.rem(z + dz, N_Z)
        remote(rs_send.at[zz], rs_recv.at[zz], rs_s.at[dz], rs_r.at[zz], r, zz * 2 + c).wait_recv()
        total = total + rs_recv[zz].astype(F32)
    mixed[...] = total

    a_send[...] = mm(slots_t, total.astype(BF)).reshape(N_DP, SLOTS, COLS).astype(BF)

    def a_start(i, carry):
        to = lax.rem(r + i, N_DP)
        remote(a_send.at[to], x.at[z, c, r], a_s.at[i], a_r.at[r], to, ep).start()
        return carry

    lax.fori_loop(1, N_DP, a_start, 0)
    x[z, c, r] = a_send[r]

    def a_wait(i, carry):
        frm = lax.rem(r + i, N_DP)
        remote(a_send.at[frm], x.at[z, c, frm], a_s.at[i], a_r.at[frm], frm, ep).wait_recv()
        return carry

    lax.fori_loop(1, N_DP, a_wait, 0)

    def g_copy(dz, zz, slot):
        return remote(x.at[slot, c], x.at[slot, c], g_s.at[dz], g_r.at[slot], r, zz * 2 + c)

    def h_copy(zz, cc):
        return remote(x.at[zz, cc], x.at[zz, cc], h_s.at[zz], h_r.at[zz], r, sib)

    for dz in (2, 1, 3):
        g_copy(dz, lax.rem(z + dz, N_Z), z).start()
    h_copy(z, c).start()

    for i in (5, 6, 7, 8):
        load[i].wait()
    square[...] = jnp.zeros_like(square)
    gate[...] = jnp.zeros_like(gate)
    upper[...] = jnp.zeros_like(upper)
    logit[...] = jnp.zeros_like(logit)

    def expert_chunk(zz):
        at = pl.multiple_of(zz * COLS, 128)
        m = x[zz].astype(F32).reshape(2 * N_DP * SLOTS, COLS)
        square[...] += jnp.sum(m * m, axis=1, keepdims=True)
        xin = (m * gain[:, pl.ds(at, COLS)]).astype(BF)
        gate[...] += mm(xin, gu[0, pl.ds(at, COLS)])
        upper[...] += mm(xin, gu[1, pl.ds(at, COLS)])
        logit[...] += lax.dot_general(
            xin, router[:, pl.ds(at, COLS)], (((1,), (1,)), ((), ())), preferred_element_type=F32)

    previous = z
    for dz in (1, 3, 2):
        zz = lax.rem(z + dz, N_Z)
        h_copy(previous, 1 - c).wait_recv()
        expert_chunk(previous)
        g_copy(dz, zz, zz).wait_recv()
        h_copy(zz, c).start()
        previous = zz
    h_copy(previous, 1 - c).wait_recv()
    expert_chunk(previous)

    scale = lax.rsqrt(square[...] * (1.0 / D) + norm_eps)
    hid[...] = (jax.nn.silu(gate[...] * scale) * (upper[...] * scale)).astype(BF)
    pick = lax.broadcasted_iota(jnp.int32, logit.shape, 1) == r
    chosen = jax.nn.sigmoid(jnp.sum(jnp.where(pick, logit[...], 0.0), axis=1, keepdims=True) * scale)

    half = N_DP * SLOTS

    def ox_copy(zz):
        return remote(ox_send.at[zz], ox_recv.at[zz], ox_s.at[zz], ox_r.at[zz], r, sib)

    def out_sum(dz):
        zz = lax.rem(z + dz, N_Z)
        ox_copy(zz).wait_recv()
        total = o_own[zz] + ox_recv[zz].astype(F32)
        if dz:
            os_send[zz] = total.astype(BF)
            remote(os_send.at[zz], os_recv.at[z], os_s.at[dz], os_r.at[z], r, zz * 2 + c).start()
        return total

    hidv = hid[...]
    for n, dz in enumerate(order):
        zz = lax.rem(z + dz, N_Z)
        block = mm(hidv, dn[:, pl.ds(pl.multiple_of(zz * COLS, 128), COLS)]) * chosen
        top, bottom = block[:half], block[half:]
        o_own[zz] = jnp.where(c == 0, top, bottom)
        ox_send[zz] = jnp.where(c == 0, bottom, top).astype(BF)
        ox_copy(zz).start()
        if n:
            out_sum(order[n - 1])
    total = out_sum(order[-1])
    for dz in (1, 3, 2):
        zz = lax.rem(z + dz, N_Z)
        remote(os_send.at[zz], os_recv.at[zz], os_s.at[dz], os_r.at[zz], r, zz * 2 + c).wait_recv()
        total = total + os_recv[zz].astype(F32)

    b_send[:, :, :COLS] = total.reshape(N_DP, SLOTS, COLS).astype(BF)
    mine = jnp.where(c == 0, chosen[:half], chosen[half:])
    high = mine.astype(BF).astype(F32)
    low = mine - high
    column = lax.broadcasted_iota(jnp.int32, (half, EXTRA), 1)
    tail = jnp.where(column == 0, high, jnp.where(column == 1, low, 0.0))
    b_send[:, :, COLS:] = tail.reshape(N_DP, SLOTS, EXTRA).astype(BF)

    def b_start(i, carry):
        to = lax.rem(r + i, N_DP)
        remote(b_send.at[to], b_recv.at[r], b_s.at[i], b_r.at[r], to, ep).start()
        return carry

    lax.fori_loop(1, N_DP, b_start, 0)
    b_recv[r] = b_send[r]

    def b_wait(i, carry):
        frm = lax.rem(r + i, N_DP)
        remote(b_send.at[frm], b_recv.at[frm], b_s.at[i], b_r.at[frm], frm, ep).wait_recv()
        return carry

    lax.fori_loop(1, N_DP, b_wait, 0)
    back = b_recv[...].astype(F32).reshape(half, COLS + EXTRA).astype(BF)
    joined = mm(slots, back)
    total_chosen = joined[:, COLS:COLS + 1] + joined[:, COLS + 1:COLS + 2]
    final = mixed[...] + joined[:, :COLS] * (route_scale / total_chosen)
    f_send[...] = final.reshape(N_Z, SPAN, COLS).astype(BF)
    for dz in (2, 1, 3):
        zz = lax.rem(z + dz, N_Z)
        remote(f_send.at[zz], f_recv.at[z], f_s.at[dz], f_r.at[z], r, zz * 2 + c).start()
    f_recv[z] = f_send[z]
    for dz in (1, 3, 2):
        zz = lax.rem(z + dz, N_Z)
        remote(f_send.at[zz], f_recv.at[zz], f_s.at[dz], f_r.at[zz], r, zz * 2 + c).wait_recv()
    for i in range(N_Z):
        out[:, i * COLS:(i + 1) * COLS] = f_recv[i]

    def drain(i, carry):
        to = lax.rem(r + i, N_DP)
        mv_copy(i).wait_send()
        remote(a_send.at[to], x.at[z, c, r], a_s.at[i], a_r.at[r], to, ep).wait_send()
        remote(b_send.at[to], b_recv.at[r], b_s.at[i], b_r.at[r], to, ep).wait_send()
        return carry

    lax.fori_loop(1, N_DP, drain, 0)
    for dz in (0, 1, 2, 3):
        zz = lax.rem(z + dz, N_Z)
        to = zz * 2 + c
        px_copy(zz).wait_send()
        ox_copy(zz).wait_send()
        h_copy(zz, c).wait_send()
        if dz:
            remote(rt.at[z], rt.at[z], rt_s.at[dz], rt_r.at[z], r, to).wait_send()
            rs_copy(dz, zz).wait_send()
            g_copy(dz, zz, z).wait_send()
            remote(os_send.at[zz], os_recv.at[z], os_s.at[dz], os_r.at[z], r, to).wait_send()
            remote(f_send.at[zz], f_recv.at[z], f_s.at[dz], f_r.at[z], r, to).wait_send()


def per_device(
    queries_c, queries_r, latents, key_rope, value_up, out_proj, norm_gain, router, gate_up, down,
    routes, lengths, plan,
):
    any_spec = pl.BlockSpec(memory_space=pl.ANY)
    smem = pl.BlockSpec(memory_space=pltpu.SMEM)
    vm = pltpu.VMEM
    dma = pltpu.SemaphoreType.DMA
    half = N_DP * SLOTS
    scratch = [
        vm((S, HEADS_HERE * LAT), BF), vm((S, HEADS_HERE * ROPE), BF), vm((S, LAT), BF), vm((ROPE, S), BF),
        vm((HEADS_HERE, LAT, VDIM), BF), vm((HEADS_HERE * VDIM, D), BF), vm((1, D), F32),
        vm((N_DP, D), BF), vm((2, D, 256), BF), vm((256, D), BF), vm((N_Z, 2, SPAN), jnp.int32),
        vm((S, HEADS_HERE * VDIM), BF), vm((N_DP, SPAN, HEADS_HERE * VDIM), BF),
        vm((N_Z, HALF, COLS), F32), vm((N_Z, HALF, COLS), BF), vm((N_Z, HALF, COLS), BF),
        vm((N_Z, HALF, COLS), BF), vm((N_Z, HALF, COLS), BF), vm((HALF, COLS), F32),
        vm((N_DP, SLOTS, COLS), BF), vm((N_Z, 2, N_DP, SLOTS, COLS), BF),
        vm((2 * half, 256), F32), vm((2 * half, 256), F32), vm((2 * half, N_DP), F32), vm((2 * half, 1), F32),
        vm((2 * half, 256), BF),
        vm((N_Z, half, COLS), F32), vm((N_Z, half, COLS), BF), vm((N_Z, half, COLS), BF),
        vm((N_Z, half, COLS), BF), vm((N_Z, half, COLS), BF),
        vm((N_DP, SLOTS, COLS + EXTRA), BF), vm((N_DP, SLOTS, COLS + EXTRA), BF),
        vm((N_Z, SPAN, COLS), BF), vm((N_Z, SPAN, COLS), BF),
        dma((9,)), dma((16,)), dma((4,)), dma((4,)), dma((16,)), dma((16,)), dma((4,)), dma((4,)),
        dma((4,)), dma((4,)), dma((16,)), dma((16,)), dma((4,)), dma((4,)), dma((4,)), dma((4,)),
        dma((4,)), dma((4,)), dma((4,)), dma((4,)), dma((16,)), dma((16,)), dma((4,)), dma((4,)),
    ]
    return pl.pallas_call(
        kernel,
        out_shape=jax.ShapeDtypeStruct((SPAN, D), BF),
        in_specs=[smem, smem] + [any_spec] * 11,
        out_specs=pl.BlockSpec(memory_space=pltpu.VMEM),
        scratch_shapes=scratch,
        compiler_params=pltpu.CompilerParams(
            collective_id=0, has_side_effects=True, vmem_limit_bytes=56 * 1024 * 1024),
        cost_estimate=pl.CostEstimate(flops=3 * 10**9, bytes_accessed=16 * 10**6, transcendentals=10**6),
    )(
        lengths, plan, queries_c, queries_r, latents, key_rope, value_up, out_proj,
        norm_gain.reshape(1, D), router.T, gate_up, down, routes.T,
    )


def solution(mesh):
    placed = (
        P("dp", "ep"),
        P("dp", "ep"),
        P("dp", None),
        P(None, "dp"),
        P("ep", None, None),
        P("ep", None),
        P(),
        P(),
        P("dp", None, None, "ep"),
        P("dp", "ep", None),
        P(("dp", "ep"), None),
        P(),
        P(),
    )
    return jax.shard_map(
        per_device, mesh=mesh, in_specs=placed, out_specs=P(("dp", "ep"), None), check_vma=False
    )
```

```python
import jax
import jax.numpy as jnp
from jax import lax
from jax.experimental import pallas as pl
from jax.experimental.pallas import tpu as pltpu
from jax.sharding import PartitionSpec as P

MESH = pl.DeviceIdType.MESH
BF = jnp.bfloat16
F32 = jnp.float32

D = 3584
LAT = 512
ROPE = 64
VDIM = 128
S = 128
SPAN = 16
HEADS_HERE = 8
N_DP = 16
N_Z = 4
HALF = 64
COLS = D // N_Z
SLOTS = 8
EXTRA = 128

softmax_scale = 192.0 ** (-0.5)
route_scale = 2.5
norm_eps = 1e-06


def mm(a, b):
    return jnp.dot(a, b, preferred_element_type=F32)


def attend(q, qr, lat, kr, position, length):
    scores = lax.dot_general(q, lat, (((1,), (1,)), ((), ())), preferred_element_type=F32)
    scores = (scores + mm(qr, kr)) * softmax_scale
    key = lax.broadcasted_iota(jnp.int32, scores.shape, 1)
    visible = (key <= position) & (key < length)
    highest = jnp.max(jnp.where(visible, scores, -jnp.inf), axis=1, keepdims=True)
    weights = jnp.where(visible, jnp.exp(scores - highest), 0.0)
    totals = jnp.sum(weights, axis=1, keepdims=True)
    mixed = mm(weights.astype(BF), lat) / totals
    return jnp.where(position[:, :1] < length, mixed, 0.0).astype(BF)


def kernel(
    lengths_s, plan_s,
    qc_h, qr_h, lat_h, kr_h, vu_h, op_h, gain_h, router_h, gu_h, dn_h, routes_h,
    out,
    qc, qr, lat, kr, vu, op, gain, router, gu, dn, rt, rt_all,
    vals, own, px_send, px_recv, rs_send, rs_recv, mixed, mv,
    a_send, x, gate, upper, logit, square, hid,
    o_own, ox_send, ox_recv, b_send, b_recv, t_send, t_recv, f_send, f_recv,
    l_sem, q_sem, in_sem, rt_s, rt_r, ra_s, ra_r, mv_s, mv_r, px_s, px_r, rs_s, rs_r, a_s, a_r, h_s, h_r,
    ox_s, ox_r, b_s, b_r, t_s, t_r, f_s, f_r,
):
    r = lax.axis_index("dp")
    ep = lax.axis_index("ep")
    z = ep // 2
    c = ep % 2
    sib = z * 2 + 1 - c

    def remote(src, dst, ssem, rsem, dp_to, ep_to):
        return pltpu.make_async_remote_copy(
            src_ref=src, dst_ref=dst, send_sem=ssem, recv_sem=rsem,
            device_id=(dp_to, ep_to), device_id_type=MESH)

    def peer(dz):
        zz = lax.rem(z + dz, N_Z)
        return zz, zz * 2 + c

    loads = [
        (lat_h, lat), (kr_h, kr), (vu_h, vu), (op_h, op), (routes_h, rt_all.at[r]),
        (gain_h, gain), (router_h, router), (gu_h.at[0], gu), (dn_h.at[0], dn),
    ]
    load = [pltpu.make_async_copy(s, d, l_sem.at[i]) for i, (s, d) in enumerate(loads)]
    qload = []
    for b in range(8):
        to = (b % 2) * HALF + (b // 2) * SPAN
        qload.append(pltpu.make_async_copy(
            qc_h.at[pl.ds(b * SPAN, SPAN)], qc.at[pl.ds(to, SPAN)], q_sem.at[b]))
        qload.append(pltpu.make_async_copy(
            qr_h.at[pl.ds(b * SPAN, SPAN)], qr.at[pl.ds(to, SPAN)], q_sem.at[8 + b]))
    load[0].start()
    load[1].start()
    for cp in qload:
        cp.start()
    for i in (2, 4, 3, 5, 6, 7, 8):
        load[i].start()

    barrier = pltpu.get_barrier_semaphore()

    def greet(i, carry):
        pl.semaphore_signal(barrier, inc=1, device_id=(lax.rem(r + i, N_DP), ep), device_id_type=MESH)
        return carry

    lax.fori_loop(1, N_DP, greet, 0)
    pl.semaphore_signal(barrier, inc=1, device_id=(r, sib), device_id_type=MESH)
    for dz in (1, 2, 3):
        pl.semaphore_signal(barrier, inc=1, device_id=(r, peer(dz)[1]), device_id_type=MESH)

    length = lengths_s[r]
    load[0].wait()
    load[1].wait()
    for cp in qload:
        cp.wait()
    latv = lat[...]
    krv = kr[...]
    place = lax.broadcasted_iota(jnp.int32, (S, S), 0)
    position = ((place % HALF) // SPAN * 2 + place // HALF) * SPAN + place % SPAN
    load[2].wait()
    for h in range(HEADS_HERE):
        att = attend(
            qc[:, h * LAT:(h + 1) * LAT], qr[:, h * ROPE:(h + 1) * ROPE], latv, krv, position, length)
        vals[:, h * VDIM:(h + 1) * VDIM] = mm(att, vu[h]).astype(BF)

    pl.semaphore_wait(barrier, N_DP - 1 + 1 + 3)
    for dz in (1, 2, 3):
        pl.semaphore_signal(in_sem, inc=1, device_id=(r, peer(dz)[1]), device_id_type=MESH)

    load[4].wait()
    last = ep == 2 * N_Z - 1

    @pl.when(last)
    def _():
        def ra_start(i, carry):
            to = lax.rem(r + i, N_DP)
            remote(rt_all.at[r], rt_all.at[r], ra_s.at[i], ra_r.at[r], to, ep).start()
            return carry

        lax.fori_loop(1, N_DP, ra_start, 0)

    load[3].wait()
    order = (2, 1, 3, 0)

    def px_copy(zz):
        return remote(px_send.at[zz], px_recv.at[zz], px_s.at[zz], px_r.at[zz], r, sib)

    def rs_copy(dz):
        zz, to = peer(dz)
        return remote(rs_send.at[zz], rs_recv.at[z], rs_s.at[dz], rs_r.at[z], r, to)

    def pair_sum(dz):
        zz, _ = peer(dz)
        px_copy(zz).wait_recv()
        total = own[zz] + px_recv[zz].astype(F32)
        if dz:
            rs_send[zz] = total.astype(BF)
            rs_copy(dz).start()
        else:
            mixed[...] = total

    valv = vals[...]
    for n, dz in enumerate(order):
        zz, _ = peer(dz)
        block = mm(valv, op[:, pl.ds(pl.multiple_of(zz * COLS, 128), COLS)])
        top, bottom = block[:HALF], block[HALF:]
        own[zz] = jnp.where(c == 0, top, bottom)
        px_send[zz] = jnp.where(c == 0, bottom, top).astype(BF)
        px_copy(zz).start()
        if n:
            pair_sum(order[n - 1])
    pair_sum(order[-1])

    @pl.when(last)
    def _():
        def ra_wait(i, carry):
            frm = lax.rem(r + i, N_DP)
            remote(rt_all.at[frm], rt_all.at[frm], ra_s.at[i], ra_r.at[frm], frm, ep).wait_recv()
            return carry

        lax.fori_loop(1, N_DP, ra_wait, 0)
        rt[z, 0] = rt_all[plan_s[r]]

    @pl.when(jnp.logical_not(last))
    def _():
        rt[z, 0] = rt_all[r]

    rt[z, 1] = rt_all[r]

    def rt_copy(dz, slot):
        return remote(rt.at[slot], rt.at[slot], rt_s.at[dz], rt_r.at[slot], r, peer(dz)[1])

    for dz in (1, 2, 3):
        rt_copy(dz, z).start()
    for dz in (1, 2, 3):
        rt_copy(dz, peer(dz)[0]).wait_recv()
    slot = lax.broadcasted_iota(jnp.int32, (N_DP * SLOTS, HALF), 0)
    row = lax.broadcasted_iota(jnp.int32, (N_DP * SLOTS, HALF), 1)
    expert = slot // SLOTS
    t_row = lax.broadcasted_iota(jnp.int32, (HALF, HALF), 0)
    t_col = lax.broadcasted_iota(jnp.int32, (HALF, HALF), 1)
    earlier = jnp.where((t_row // SPAN == t_col // SPAN) & (t_row < t_col), 1.0, 0.0).astype(BF)
    same = (slot // 2) % N_Z == row // SPAN

    def slot_matrix(which):
        first = jnp.concatenate([rt[i, which, 0:1, :] for i in range(N_Z)], axis=1)
        second = jnp.concatenate([rt[i, which, 1:2, :] for i in range(N_Z)], axis=1)
        named = jnp.where((first == expert) | (second == expert), 1.0, 0.0)
        before = mm(named.astype(BF), earlier)
        return jnp.where(same & (before == (slot % 2).astype(F32)), named, 0.0)

    slots_t = slot_matrix(0).astype(BF)

    total = mixed[...]
    for dz in (1, 3, 2):
        zz, to = peer(dz)
        remote(rs_send.at[zz], rs_recv.at[zz], rs_s.at[dz], rs_r.at[zz], r, to).wait_recv()
        total = total + rs_recv[zz].astype(F32)
    mixed[...] = total

    a_send[...] = mm(slots_t, total.astype(BF)).reshape(N_DP, SLOTS, COLS).astype(BF)
    pl.semaphore_wait(in_sem, 3)

    def a_copy(to, dz):
        return remote(a_send.at[to], x.at[z, c, r], a_s.at[dz], a_r.at[z], to, peer(dz)[1])

    def a_start(i, carry):
        to = lax.rem(r + i, N_DP)
        for dz in range(N_Z):
            a_copy(to, dz).start()
        return carry

    for dz in (1, 2, 3):
        a_copy(r, dz).start()
    lax.fori_loop(1, N_DP, a_start, 0)
    x[z, c, r] = a_send[r]

    def a_wait(zz, count):
        part = x.at[zz, c, pl.ds(0, count)]
        remote(part, part, a_s.at[0], a_r.at[zz], r, sib).wait_recv()

    def h_copy(zz, cc):
        return remote(x.at[zz, cc], x.at[zz, cc], h_s.at[zz], h_r.at[zz], r, sib)

    for i in (5, 6, 7, 8):
        load[i].wait()
    square[...] = jnp.zeros_like(square)
    gate[...] = jnp.zeros_like(gate)
    upper[...] = jnp.zeros_like(upper)
    logit[...] = jnp.zeros_like(logit)

    def expert_chunk(zz):
        at = pl.multiple_of(zz * COLS, 128)
        m = x[zz].astype(F32).reshape(2 * N_DP * SLOTS, COLS)
        square[...] += jnp.sum(m * m, axis=1, keepdims=True)
        xin = (m * gain[:, pl.ds(at, COLS)]).astype(BF)
        gate[...] += mm(xin, gu[0, pl.ds(at, COLS)])
        upper[...] += mm(xin, gu[1, pl.ds(at, COLS)])
        logit[...] += lax.dot_general(
            xin, router[:, pl.ds(at, COLS)], (((1,), (1,)), ((), ())), preferred_element_type=F32)

    previous = None
    for dz in (0, 1, 3, 2):
        zz, _ = peer(dz)
        a_wait(zz, N_DP if dz else N_DP - 1)
        h_copy(zz, c).start()
        if previous is not None:
            h_copy(previous, 1 - c).wait_recv()
            expert_chunk(previous)
        previous = zz
    h_copy(previous, 1 - c).wait_recv()
    expert_chunk(previous)

    def mv_start(i, carry):
        to = lax.rem(r + i, N_DP)
        remote(mv.at[r], mv.at[r], mv_s.at[0], mv_r.at[0], to, ep).start()
        return carry

    @pl.when(c == 1)
    def _():
        mv[r] = mixed[HALF - SPAN:].astype(BF)
        lax.fori_loop(1, N_DP, mv_start, 0)

    scale = lax.rsqrt(square[...] * (1.0 / D) + norm_eps)
    hidv = (jax.nn.silu(gate[...] * scale) * (upper[...] * scale)).astype(BF)
    pick = lax.broadcasted_iota(jnp.int32, logit.shape, 1) == r
    chosen = jax.nn.sigmoid(jnp.sum(jnp.where(pick, logit[...], 0.0), axis=1, keepdims=True) * scale)

    half = N_DP * SLOTS
    to_row = lax.broadcasted_iota(jnp.int32, (2 * half, 2 * half), 0)
    from_row = lax.broadcasted_iota(jnp.int32, (2 * half, 2 * half), 1)
    rank = (to_row % half) // SLOTS
    partner = jnp.zeros_like(rank)
    for i in range(N_DP):
        partner = jnp.where(rank == i, plan_s[i], partner)
    moves = (to_row >= half) & (to_row % SLOTS >= SLOTS - 2)
    wanted = to_row + jnp.where(moves, (partner - rank) * SLOTS, 0)
    swap = jnp.where(from_row == wanted, 1.0, 0.0).astype(BF)
    hid[...] = mm(swap, hidv).astype(BF)
    column = lax.broadcasted_iota(jnp.int32, (2 * half, EXTRA), 1)
    high = chosen.astype(BF).astype(F32)
    tail = jnp.where(column == 0, high, jnp.where(column == 1, chosen - high, 0.0)).astype(BF)
    tail = mm(swap, tail)
    chosen = tail[:, 0:1] + tail[:, 1:2]
    t_send[...] = jnp.where(c == 0, tail[:half], tail[half:]).reshape(N_DP, SLOTS, EXTRA).astype(BF)

    def t_start(i, carry):
        to = lax.rem(r + i, N_DP)
        remote(t_send.at[to], t_recv.at[r], t_s.at[0], t_r.at[0], to, ep).start()
        return carry

    lax.fori_loop(1, N_DP, t_start, 0)
    t_recv[r] = t_send[r]

    def ox_copy(zz):
        return remote(ox_send.at[zz], ox_recv.at[zz], ox_s.at[zz], ox_r.at[zz], r, sib)

    def out_sum(dz):
        zz, to_ep = peer(dz)
        ox_copy(zz).wait_recv()
        total = o_own[zz] + ox_recv[zz].astype(F32)
        b_send[zz] = total.reshape(N_DP, SLOTS, COLS).astype(BF)

        def b_start(i, carry):
            to = lax.rem(r + i, N_DP)
            remote(b_send.at[zz, to], b_recv.at[z, r], b_s.at[dz], b_r.at[z], to, to_ep).start()
            return carry

        lax.fori_loop(0 if dz else 1, N_DP, b_start, 0)
        if dz == 0:
            b_recv[z, r] = b_send[z, r]

    hidv = hid[...]
    for n, dz in enumerate(order):
        zz, _ = peer(dz)
        block = mm(hidv, dn[:, pl.ds(pl.multiple_of(zz * COLS, 128), COLS)]) * chosen
        top, bottom = block[:half], block[half:]
        o_own[zz] = jnp.where(c == 0, top, bottom)
        ox_send[zz] = jnp.where(c == 0, bottom, top).astype(BF)
        ox_copy(zz).start()
        if n:
            out_sum(order[n - 1])
    out_sum(order[-1])

    def mv_all():
        part = mv.at[pl.ds(0, N_DP - 1)]
        return remote(part, part, mv_s.at[0], mv_r.at[0], r, sib)

    @pl.when(c == 1)
    def _():
        mv_all().wait_recv()
        mixed[HALF - SPAN:, :] = mv[plan_s[r]].astype(F32)

    slots = slot_matrix(1).T.astype(BF)
    t_part = t_recv.at[pl.ds(0, N_DP - 1)]
    remote(t_part, t_part, t_s.at[0], t_r.at[0], r, sib).wait_recv()
    weight = mm(slots, t_recv[...].astype(F32).reshape(half, EXTRA).astype(BF))
    factor = route_scale / (weight[:, 0:1] + weight[:, 1:2])
    joined = jnp.zeros((HALF, COLS), F32)
    for dz in (0, 1, 3, 2):
        zz, _ = peer(dz)
        part = b_recv.at[zz, pl.ds(0, N_DP if dz else N_DP - 1)]
        remote(part, part, b_s.at[0], b_r.at[zz], r, sib).wait_recv()
        joined = joined + mm(slots, b_recv[zz].astype(F32).reshape(half, COLS).astype(BF))
    final = mixed[...] + joined * factor
    f_send[...] = final.reshape(N_Z, SPAN, COLS).astype(BF)

    def f_copy(dz):
        zz, to = peer(dz)
        return remote(f_send.at[zz], f_recv.at[z], f_s.at[dz], f_r.at[z], r, to)

    for dz in (2, 1, 3):
        f_copy(dz).start()
    f_recv[z] = f_send[z]
    for dz in (1, 3, 2):
        zz, to = peer(dz)
        remote(f_send.at[zz], f_recv.at[zz], f_s.at[dz], f_r.at[zz], r, to).wait_recv()
    for i in range(N_Z):
        out[:, i * COLS:(i + 1) * COLS] = f_recv[i]

    for dz in range(N_Z):
        zz, to = peer(dz)
        count = N_DP if dz else N_DP - 1
        part = b_send.at[zz, pl.ds(0, count)]
        remote(part, part, b_s.at[dz], b_r.at[zz], r, sib).wait_send()
        part = a_send.at[pl.ds(0, count)]
        remote(part, part, a_s.at[dz], a_r.at[zz], r, sib).wait_send()
        px_copy(zz).wait_send()
        ox_copy(zz).wait_send()
        h_copy(zz, c).wait_send()
        if dz:
            rt_copy(dz, z).wait_send()
            rs_copy(dz).wait_send()
            f_copy(dz).wait_send()
    remote(t_part, t_part, t_s.at[0], t_r.at[0], r, sib).wait_send()

    @pl.when(c == 1)
    def _():
        mv_all().wait_send()

    @pl.when(last)
    def _():
        def ra_drain(i, carry):
            to = lax.rem(r + i, N_DP)
            remote(rt_all.at[r], rt_all.at[r], ra_s.at[i], ra_r.at[r], to, ep).wait_send()
            return carry

        lax.fori_loop(1, N_DP, ra_drain, 0)


def per_device(
    queries_c, queries_r, latents, key_rope, value_up, out_proj, norm_gain, router, gate_up, down,
    routes, lengths, plan,
):
    any_spec = pl.BlockSpec(memory_space=pl.ANY)
    smem = pl.BlockSpec(memory_space=pltpu.SMEM)
    vm = pltpu.VMEM
    dma = pltpu.SemaphoreType.DMA
    half = N_DP * SLOTS
    scratch = [
        vm((S, HEADS_HERE * LAT), BF), vm((S, HEADS_HERE * ROPE), BF), vm((S, LAT), BF), vm((ROPE, S), BF),
        vm((HEADS_HERE, LAT, VDIM), BF), vm((HEADS_HERE * VDIM, D), BF), vm((1, D), F32),
        vm((N_DP, D), BF), vm((2, D, 256), BF), vm((256, D), BF),
        vm((N_Z, 2, 2, SPAN), jnp.int32), vm((N_DP, 2, SPAN), jnp.int32),
        vm((S, HEADS_HERE * VDIM), BF),
        vm((N_Z, HALF, COLS), F32), vm((N_Z, HALF, COLS), BF), vm((N_Z, HALF, COLS), BF),
        vm((N_Z, HALF, COLS), BF), vm((N_Z, HALF, COLS), BF), vm((HALF, COLS), F32),
        vm((N_DP, SPAN, COLS), BF),
        vm((N_DP, SLOTS, COLS), BF), vm((N_Z, 2, N_DP, SLOTS, COLS), BF),
        vm((2 * half, 256), F32), vm((2 * half, 256), F32), vm((2 * half, N_DP), F32), vm((2 * half, 1), F32),
        vm((2 * half, 256), BF),
        vm((N_Z, half, COLS), F32), vm((N_Z, half, COLS), BF), vm((N_Z, half, COLS), BF),
        vm((N_Z, N_DP, SLOTS, COLS), BF), vm((N_Z, N_DP, SLOTS, COLS), BF),
        vm((N_DP, SLOTS, EXTRA), BF), vm((N_DP, SLOTS, EXTRA), BF),
        vm((N_Z, SPAN, COLS), BF), vm((N_Z, SPAN, COLS), BF),
        dma((9,)), dma((16,)), pltpu.SemaphoreType.REGULAR, dma((4,)), dma((4,)), dma((16,)), dma((16,)),
        dma((1,)), dma((1,)), dma((4,)), dma((4,)), dma((4,)), dma((4,)), dma((4,)), dma((4,)),
        dma((4,)), dma((4,)), dma((4,)), dma((4,)), dma((4,)), dma((4,)), dma((1,)), dma((1,)),
        dma((4,)), dma((4,)),
    ]
    return pl.pallas_call(
        kernel,
        out_shape=jax.ShapeDtypeStruct((SPAN, D), BF),
        in_specs=[smem, smem] + [any_spec] * 11,
        out_specs=pl.BlockSpec(memory_space=pltpu.VMEM),
        scratch_shapes=scratch,
        compiler_params=pltpu.CompilerParams(
            collective_id=0, has_side_effects=True, vmem_limit_bytes=56 * 1024 * 1024),
        cost_estimate=pl.CostEstimate(flops=3 * 10**9, bytes_accessed=16 * 10**6, transcendentals=10**6),
    )(
        lengths, plan, queries_c, queries_r, latents, key_rope, value_up, out_proj,
        norm_gain.reshape(1, D), router.T, gate_up, down, routes.T,
    )


def solution(mesh):
    placed = (
        P("dp", "ep"),
        P("dp", "ep"),
        P("dp", None),
        P(None, "dp"),
        P("ep", None, None),
        P("ep", None),
        P(),
        P(),
        P("dp", None, None, "ep"),
        P("dp", "ep", None),
        P(("dp", "ep"), None),
        P(),
        P(),
    )
    return jax.shard_map(
        per_device, mesh=mesh, in_specs=placed, out_specs=P(("dp", "ep"), None), check_vma=False
    )
```

```python
import jax
import jax.numpy as jnp
from jax import lax
from jax.experimental import pallas as pl
from jax.experimental.pallas import tpu as pltpu
from jax.sharding import PartitionSpec as P

MESH = pl.DeviceIdType.MESH
BF = jnp.bfloat16
F32 = jnp.float32

D = 3584
LAT = 512
ROPE = 64
VDIM = 128
S = 128
SPAN = 16
HEADS_HERE = 8
N_DP = 16
N_Z = 4
HALF = 64
COLS = D // N_Z
SLOTS = 8
EXTRA = 128

softmax_scale = 192.0 ** (-0.5)
route_scale = 2.5
norm_eps = 1e-06


def mm(a, b):
    return jnp.dot(a, b, preferred_element_type=F32)


def attend(q, qr, lat, kr, position, length):
    scores = lax.dot_general(q, lat, (((1,), (1,)), ((), ())), preferred_element_type=F32)
    scores = (scores + mm(qr, kr)) * softmax_scale
    key = lax.broadcasted_iota(jnp.int32, scores.shape, 1)
    visible = (key <= position) & (key < length)
    highest = jnp.max(jnp.where(visible, scores, -jnp.inf), axis=1, keepdims=True)
    weights = jnp.where(visible, jnp.exp(scores - highest), 0.0)
    totals = jnp.sum(weights, axis=1, keepdims=True)
    mixed = mm(weights.astype(BF), lat) / totals
    return jnp.where(position[:, :1] < length, mixed, 0.0).astype(BF)


def kernel(
    lengths_h, plan_h, qc_h, qr_h, lat_h, kr_h, vu_h, op_h, gain_h, router_h, gu_h, dn_h, routes_h,
    out,
    lengths_s, plan_s, qc, qr, lat, kr, vu, op, gain, router, gu, dn, rt, rt_all,
    vals, own, px_send, px_recv, rs_send, rs_recv, mixed,
    a_send, x, gate, upper, logit, square, hid,
    o_own, residual, ox_send, ox_recv, b_send, b_recv, t_send, t_recv, f_send, f_recv,
    l_sem, q_sem, o_sem, in_sem, rt_s, rt_r, ra_s, ra_r, px_s, px_r, rs_s, rs_r, a_s, a_r, h_s, h_r,
    ox_s, ox_r, b_s, b_r, t_s, t_r, f_s, f_r,
):
    r = lax.axis_index("dp")
    ep = lax.axis_index("ep")
    z = ep // 2
    c = ep % 2
    sib = z * 2 + 1 - c

    def remote(src, dst, ssem, rsem, dp_to, ep_to):
        return pltpu.make_async_remote_copy(
            src_ref=src, dst_ref=dst, send_sem=ssem, recv_sem=rsem,
            device_id=(dp_to, ep_to), device_id_type=MESH)

    def peer(dz):
        zz = lax.rem(z + dz, N_Z)
        return zz, zz * 2 + c

    barrier = pltpu.get_barrier_semaphore()

    def greet(i, carry):
        pl.semaphore_signal(barrier, inc=1, device_id=(lax.rem(r + i, N_DP), ep), device_id_type=MESH)
        return carry

    lax.fori_loop(1, N_DP, greet, 0)
    pl.semaphore_signal(barrier, inc=1, device_id=(r, sib), device_id_type=MESH)
    for dz in (1, 2, 3):
        pl.semaphore_signal(barrier, inc=1, device_id=(r, peer(dz)[1]), device_id_type=MESH)

    loads = [
        (lat_h, lat), (kr_h, kr), (vu_h, vu), (op_h, op), (routes_h, rt_all.at[r]),
        (gain_h, gain), (router_h, router), (gu_h.at[0], gu), (dn_h.at[0], dn), (lengths_h, lengths_s), (plan_h, plan_s),
    ]
    load = [pltpu.make_async_copy(s, d, l_sem.at[i]) for i, (s, d) in enumerate(loads)]
    qload = []
    for b in range(8):
        to = (b % 2) * HALF + (b // 2) * SPAN
        qload.append(pltpu.make_async_copy(
            qc_h.at[pl.ds(b * SPAN, SPAN)], qc.at[pl.ds(to, SPAN)], q_sem.at[b]))
        qload.append(pltpu.make_async_copy(
            qr_h.at[pl.ds(b * SPAN, SPAN)], qr.at[pl.ds(to, SPAN)], q_sem.at[8 + b]))
    load[9].start()
    load[0].start()
    load[1].start()
    for cp in qload:
        cp.start()
    load[2].start()

    load[0].wait()
    load[1].wait()
    for cp in qload:
        cp.wait()
    for i in (3, 4, 10, 5, 6, 7, 8):
        load[i].start()
    load[9].wait()
    length = lengths_s[r]
    latv = lat[...]
    krv = kr[...]
    place = lax.broadcasted_iota(jnp.int32, (S, S), 0)
    position = ((place % HALF) // SPAN * 2 + place // HALF) * SPAN + place % SPAN
    load[2].wait()
    for h in range(HEADS_HERE):
        att = attend(
            qc[:, h * LAT:(h + 1) * LAT], qr[:, h * ROPE:(h + 1) * ROPE], latv, krv, position, length)
        vals[:, h * VDIM:(h + 1) * VDIM] = mm(att, vu[h]).astype(BF)

    pl.semaphore_wait(barrier, N_DP - 1 + 1 + 3)
    for dz in (1, 2, 3):
        pl.semaphore_signal(in_sem, inc=1, device_id=(r, peer(dz)[1]), device_id_type=MESH)

    load[4].wait()
    load[10].wait()
    last = ep == 2 * N_Z - 1

    @pl.when(last)
    def _():
        def ra_start(i, carry):
            to = lax.rem(r + i, N_DP)
            remote(rt_all.at[r], rt_all.at[r], ra_s.at[i], ra_r.at[r], to, ep).start()
            return carry

        lax.fori_loop(1, N_DP, ra_start, 0)

    load[3].wait()
    order = (2, 1, 3, 0)

    def px_copy(zz):
        return remote(px_send.at[zz], px_recv.at[zz], px_s.at[zz], px_r.at[zz], r, sib)

    def rs_copy(dz):
        zz, to = peer(dz)
        return remote(rs_send.at[zz], rs_recv.at[z], rs_s.at[dz], rs_r.at[z], r, to)

    def pair_sum(dz):
        zz, _ = peer(dz)
        px_copy(zz).wait_recv()
        total = own[zz] + px_recv[zz].astype(F32)
        if dz:
            rs_send[zz] = total.astype(BF)
            rs_copy(dz).start()
        else:
            mixed[...] = total

    valv = vals[...]
    for n, dz in enumerate(order):
        zz, _ = peer(dz)
        block = mm(valv, op[:, pl.ds(pl.multiple_of(zz * COLS, 128), COLS)])
        top, bottom = block[:HALF], block[HALF:]
        own[zz] = jnp.where(c == 0, top, bottom)
        px_send[zz] = jnp.where(c == 0, bottom, top).astype(BF)
        px_copy(zz).start()
        if n:
            pair_sum(order[n - 1])
    pair_sum(order[-1])

    @pl.when(last)
    def _():
        def ra_wait(i, carry):
            frm = lax.rem(r + i, N_DP)
            remote(rt_all.at[frm], rt_all.at[frm], ra_s.at[i], ra_r.at[frm], frm, ep).wait_recv()
            return carry

        lax.fori_loop(1, N_DP, ra_wait, 0)
        rt[z, 0] = rt_all[plan_s[r]]

    @pl.when(jnp.logical_not(last))
    def _():
        rt[z, 0] = rt_all[r]

    rt[z, 1] = rt_all[r]

    def rt_copy(dz, slot):
        return remote(rt.at[slot], rt.at[slot], rt_s.at[dz], rt_r.at[slot], r, peer(dz)[1])

    for dz in (1, 2, 3):
        rt_copy(dz, z).start()
    for dz in (1, 2, 3):
        rt_copy(dz, peer(dz)[0]).wait_recv()
    slot = lax.broadcasted_iota(jnp.int32, (N_DP * SLOTS, HALF), 0)
    row = lax.broadcasted_iota(jnp.int32, (N_DP * SLOTS, HALF), 1)
    expert = slot // SLOTS
    t_row = lax.broadcasted_iota(jnp.int32, (HALF, HALF), 0)
    t_col = lax.broadcasted_iota(jnp.int32, (HALF, HALF), 1)
    earlier = jnp.where((t_row // SPAN == t_col // SPAN) & (t_row < t_col), 1.0, 0.0).astype(BF)
    same = (slot // 2) % N_Z == row // SPAN

    def slot_matrix(which):
        first = jnp.concatenate([rt[i, which, 0:1, :] for i in range(N_Z)], axis=1)
        second = jnp.concatenate([rt[i, which, 1:2, :] for i in range(N_Z)], axis=1)
        named = jnp.where((first == expert) | (second == expert), 1.0, 0.0)
        before = mm(named.astype(BF), earlier)
        return jnp.where(same & (before == (slot % 2).astype(F32)), named, 0.0)

    slots_t = slot_matrix(0).astype(BF)

    total = mixed[...]
    for dz in (1, 3, 2):
        zz, to = peer(dz)
        remote(rs_send.at[zz], rs_recv.at[zz], rs_s.at[dz], rs_r.at[zz], r, to).wait_recv()
        total = total + rs_recv[zz].astype(F32)

    a_send[...] = mm(slots_t, total.astype(BF)).reshape(N_DP, SLOTS, COLS).astype(BF)
    pl.semaphore_wait(in_sem, 3)

    def a_copy(to, dz):
        return remote(a_send.at[to], x.at[z, c, r], a_s.at[dz], a_r.at[z], to, peer(dz)[1])

    def a_start(i, carry):
        to = lax.rem(r + i, N_DP)
        for dz in range(N_Z):
            a_copy(to, dz).start()
        return carry

    for dz in (1, 2, 3):
        a_copy(r, dz).start()
    lax.fori_loop(1, N_DP, a_start, 0)
    x[z, c, r] = a_send[r]

    def a_wait(zz, count):
        part = x.at[zz, c, pl.ds(0, count)]
        remote(part, part, a_s.at[0], a_r.at[zz], r, sib).wait_recv()

    def h_copy(zz, cc):
        return remote(x.at[zz, cc], x.at[zz, cc], h_s.at[zz], h_r.at[zz], r, sib)

    for i in (5, 6, 7, 8):
        load[i].wait()
    square[...] = jnp.zeros_like(square)
    gate[...] = jnp.zeros_like(gate)
    upper[...] = jnp.zeros_like(upper)
    logit[...] = jnp.zeros_like(logit)

    def expert_chunk(zz):
        at = pl.multiple_of(zz * COLS, 128)
        m = x[zz].astype(F32).reshape(2 * N_DP * SLOTS, COLS)
        square[...] += jnp.sum(m * m, axis=1, keepdims=True)
        xin = (m * gain[pl.ds(at, COLS)].reshape(1, COLS)).astype(BF)
        gate[...] += mm(xin, gu[0, pl.ds(at, COLS)])
        upper[...] += mm(xin, gu[1, pl.ds(at, COLS)])
        logit[...] += lax.dot_general(
            xin, router[:, pl.ds(at, COLS)], (((1,), (1,)), ((), ())), preferred_element_type=F32)

    previous = None
    for dz in (0, 1, 3, 2):
        zz, _ = peer(dz)
        a_wait(zz, N_DP if dz else N_DP - 1)
        h_copy(zz, c).start()
        if previous is not None:
            h_copy(previous, 1 - c).wait_recv()
            expert_chunk(previous)
        previous = zz
    h_copy(previous, 1 - c).wait_recv()
    expert_chunk(previous)

    scale = lax.rsqrt(square[...] * (1.0 / D) + norm_eps)
    hidv = (jax.nn.silu(gate[...] * scale) * (upper[...] * scale)).astype(BF)
    pick = lax.broadcasted_iota(jnp.int32, logit.shape, 1) == r
    chosen = jax.nn.sigmoid(jnp.sum(jnp.where(pick, logit[...], 0.0), axis=1, keepdims=True) * scale)

    half = N_DP * SLOTS
    to_row = lax.broadcasted_iota(jnp.int32, (2 * half, 2 * half), 0)
    from_row = lax.broadcasted_iota(jnp.int32, (2 * half, 2 * half), 1)
    rank = (to_row % half) // SLOTS
    partner = jnp.zeros_like(rank)
    for i in range(N_DP):
        partner = jnp.where(rank == i, plan_s[i], partner)
    moves = (to_row >= half) & (to_row % SLOTS >= SLOTS - 2)
    wanted = to_row + jnp.where(moves, (partner - rank) * SLOTS, 0)
    swap = jnp.where(from_row == wanted, 1.0, 0.0).astype(BF)
    hid[...] = mm(swap, hidv).astype(BF)
    column = lax.broadcasted_iota(jnp.int32, (2 * half, EXTRA), 1)
    high = chosen.astype(BF).astype(F32)
    tail = jnp.where(column == 0, high, jnp.where(column == 1, chosen - high, 0.0)).astype(BF)
    tail = mm(swap, tail)
    chosen = tail[:, 0:1] + tail[:, 1:2]
    t_send[...] = jnp.where(c == 0, tail[:half], tail[half:]).reshape(N_DP, SLOTS, EXTRA).astype(BF)

    def t_start(i, carry):
        to = lax.rem(r + i, N_DP)
        remote(t_send.at[to], t_recv.at[r], t_s.at[0], t_r.at[0], to, ep).start()
        return carry

    lax.fori_loop(1, N_DP, t_start, 0)
    t_recv[r] = t_send[r]

    swap_half = jnp.where(c == 0, swap[:half, :half], swap[half:, half:])
    mine = jnp.where(c == 0, chosen[:half], chosen[half:]) * (1.0 / route_scale)
    residual[...] = mm(swap_half, x[z, c].astype(F32).reshape(half, COLS).astype(BF)) * mine

    def ox_copy(zz):
        return remote(ox_send.at[zz], ox_recv.at[zz], ox_s.at[zz], ox_r.at[zz], r, sib)

    def out_sum(dz):
        zz, to_ep = peer(dz)
        ox_copy(zz).wait_recv()
        total = o_own[zz] + ox_recv[zz].astype(F32)
        if dz == 0:
            total = total + residual[...]
        b_send[zz] = total.reshape(N_DP, SLOTS, COLS).astype(BF)

        def b_start(i, carry):
            to = lax.rem(r + i, N_DP)
            remote(b_send.at[zz, to], b_recv.at[z, r], b_s.at[dz], b_r.at[z], to, to_ep).start()
            return carry

        lax.fori_loop(0 if dz else 1, N_DP, b_start, 0)
        if dz == 0:
            b_recv[z, r] = b_send[z, r]

    hidv = hid[...]
    for n, dz in enumerate(order):
        zz, _ = peer(dz)
        block = mm(hidv, dn[:, pl.ds(pl.multiple_of(zz * COLS, 128), COLS)]) * chosen
        top, bottom = block[:half], block[half:]
        o_own[zz] = jnp.where(c == 0, top, bottom)
        ox_send[zz] = jnp.where(c == 0, bottom, top).astype(BF)
        ox_copy(zz).start()
        if n:
            out_sum(order[n - 1])
    out_sum(order[-1])

    slots = slot_matrix(1).T.astype(BF)
    t_part = t_recv.at[pl.ds(0, N_DP - 1)]
    remote(t_part, t_part, t_s.at[0], t_r.at[0], r, sib).wait_recv()
    weight = mm(slots, t_recv[...].astype(F32).reshape(half, EXTRA).astype(BF))
    factor = route_scale / (weight[:, 0:1] + weight[:, 1:2])
    joined = jnp.zeros((HALF, COLS), F32)
    for dz in (0, 1, 3, 2):
        zz, _ = peer(dz)
        part = b_recv.at[zz, pl.ds(0, N_DP if dz else N_DP - 1)]
        remote(part, part, b_s.at[0], b_r.at[zz], r, sib).wait_recv()
        joined = joined + mm(slots, b_recv[zz].astype(F32).reshape(half, COLS).astype(BF))
    final = joined * factor
    f_send[...] = final.reshape(N_Z, SPAN, COLS).astype(BF)

    def f_copy(dz):
        zz, to = peer(dz)
        return remote(f_send.at[zz], f_recv.at[z], f_s.at[dz], f_r.at[z], r, to)

    for dz in (2, 1, 3):
        f_copy(dz).start()
    f_recv[z] = f_send[z]

    def store(zz):
        columns = pl.ds(pl.multiple_of(zz * COLS, 128), COLS)
        return pltpu.make_async_copy(f_recv.at[zz], out.at[:, columns], o_sem.at[zz])

    store(z).start()
    for dz in (1, 3, 2):
        zz, to = peer(dz)
        remote(f_send.at[zz], f_recv.at[zz], f_s.at[dz], f_r.at[zz], r, to).wait_recv()
        store(zz).start()

    for i in range(N_Z):
        store(i).wait()
    for dz in range(N_Z):
        zz, to = peer(dz)
        count = N_DP if dz else N_DP - 1
        part = b_send.at[zz, pl.ds(0, count)]
        remote(part, part, b_s.at[dz], b_r.at[zz], r, sib).wait_send()
        part = a_send.at[pl.ds(0, count)]
        remote(part, part, a_s.at[dz], a_r.at[zz], r, sib).wait_send()
        px_copy(zz).wait_send()
        ox_copy(zz).wait_send()
        h_copy(zz, c).wait_send()
        if dz:
            rt_copy(dz, z).wait_send()
            rs_copy(dz).wait_send()
            f_copy(dz).wait_send()
    remote(t_part, t_part, t_s.at[0], t_r.at[0], r, sib).wait_send()

    @pl.when(last)
    def _():
        def ra_drain(i, carry):
            to = lax.rem(r + i, N_DP)
            remote(rt_all.at[r], rt_all.at[r], ra_s.at[i], ra_r.at[r], to, ep).wait_send()
            return carry

        lax.fori_loop(1, N_DP, ra_drain, 0)


def per_device(
    queries_c, queries_r, latents, key_rope, value_up, out_proj, norm_gain, router, gate_up, down,
    routes, lengths, plan,
):
    any_spec = pl.BlockSpec(memory_space=pl.ANY)
    vm = pltpu.VMEM
    dma = pltpu.SemaphoreType.DMA
    half = N_DP * SLOTS
    scratch = [
        pltpu.SMEM((N_DP,), jnp.int32), pltpu.SMEM((N_DP,), jnp.int32),
        vm((S, HEADS_HERE * LAT), BF), vm((S, HEADS_HERE * ROPE), BF), vm((S, LAT), BF), vm((ROPE, S), BF),
        vm((HEADS_HERE, LAT, VDIM), BF), vm((HEADS_HERE * VDIM, D), BF), vm((D,), F32),
        vm((N_DP, D), BF), vm((2, D, 256), BF), vm((256, D), BF),
        vm((N_Z, 2, 2, SPAN), jnp.int32), vm((N_DP, 2, SPAN), jnp.int32),
        vm((S, HEADS_HERE * VDIM), BF),
        vm((N_Z, HALF, COLS), F32), vm((N_Z, HALF, COLS), BF), vm((N_Z, HALF, COLS), BF),
        vm((N_Z, HALF, COLS), BF), vm((N_Z, HALF, COLS), BF), vm((HALF, COLS), F32),
        vm((N_DP, SLOTS, COLS), BF), vm((N_Z, 2, N_DP, SLOTS, COLS), BF),
        vm((2 * half, 256), F32), vm((2 * half, 256), F32), vm((2 * half, N_DP), F32), vm((2 * half, 1), F32),
        vm((2 * half, 256), BF),
        vm((N_Z, half, COLS), F32), vm((half, COLS), F32), vm((N_Z, half, COLS), BF), vm((N_Z, half, COLS), BF),
        vm((N_Z, N_DP, SLOTS, COLS), BF), vm((N_Z, N_DP, SLOTS, COLS), BF),
        vm((N_DP, SLOTS, EXTRA), BF), vm((N_DP, SLOTS, EXTRA), BF),
        vm((N_Z, SPAN, COLS), BF), vm((N_Z, SPAN, COLS), BF),
        dma((11,)), dma((16,)), dma((4,)), pltpu.SemaphoreType.REGULAR, dma((4,)), dma((4,)), dma((16,)), dma((16,)),
        dma((4,)), dma((4,)), dma((4,)), dma((4,)), dma((4,)), dma((4,)),
        dma((4,)), dma((4,)), dma((4,)), dma((4,)), dma((4,)), dma((4,)), dma((1,)), dma((1,)),
        dma((4,)), dma((4,)),
    ]
    return pl.pallas_call(
        kernel,
        out_shape=jax.ShapeDtypeStruct((SPAN, D), BF),
        in_specs=[any_spec] * 13,
        out_specs=any_spec,
        scratch_shapes=scratch,
        compiler_params=pltpu.CompilerParams(
            collective_id=0, has_side_effects=True, vmem_limit_bytes=56 * 1024 * 1024),
        cost_estimate=pl.CostEstimate(flops=3 * 10**9, bytes_accessed=16 * 10**6, transcendentals=10**6),
    )(
        lengths, plan, queries_c, queries_r, latents, key_rope, value_up, out_proj,
        norm_gain, router.T, gate_up, down, routes.T,
    )


def solution(mesh):
    placed = (
        P("dp", "ep"),
        P("dp", "ep"),
        P("dp", None),
        P(None, "dp"),
        P("ep", None, None),
        P("ep", None),
        P(),
        P(),
        P("dp", None, None, "ep"),
        P("dp", "ep", None),
        P(("dp", "ep"), None),
        P(),
        P(),
    )
    return jax.shard_map(
        per_device, mesh=mesh, in_specs=placed, out_specs=P(("dp", "ep"), None), check_vma=False
    )
```

```python
import jax
import jax.numpy as jnp
from jax import lax
from jax.experimental import pallas as pl
from jax.experimental.pallas import tpu as pltpu
from jax.sharding import PartitionSpec as P

MESH = pl.DeviceIdType.MESH
BF = jnp.bfloat16
F32 = jnp.float32

D = 3584
LAT = 512
ROPE = 64
VDIM = 128
S = 128
SPAN = 16
HEADS_HERE = 8
N_DP = 16
N_Z = 4
HALF = 64
COLS = D // N_Z
SLOTS = 8
EXTRA = 128
LAG = 2
PIECES = ((0, 384), (384, 512))

softmax_scale = 192.0 ** (-0.5)
route_scale = 2.5
norm_eps = 1e-06


def mm(a, b):
    return jnp.dot(a, b, preferred_element_type=F32)


def attend(q, qr, lat, kr, position, length):
    scores = lax.dot_general(q, lat, (((1,), (1,)), ((), ())), preferred_element_type=F32)
    scores = (scores + mm(qr, kr)) * softmax_scale
    key = lax.broadcasted_iota(jnp.int32, scores.shape, 1)
    visible = (key <= position) & (key < length)
    highest = jnp.max(jnp.where(visible, scores, -jnp.inf), axis=1, keepdims=True)
    weights = jnp.where(visible, jnp.exp(scores - highest), 0.0)
    totals = jnp.sum(weights, axis=1, keepdims=True)
    mixed = mm(weights.astype(BF), lat) / totals
    return jnp.where(position[:, :1] < length, mixed, 0.0).astype(BF)


def kernel(
    lengths_h, plan_h, qc_h, qr_h, lat_h, kr_h, vu_h, op_h, gain_h, router_h, gu_h, dn_h, routes_h,
    out,
    lengths_s, plan_s, qc, qr, lat, kr, vu, op, gain, router, gu, dn, rt, rt_all, rt_last,
    vals, gate, upper, logit, square, swap,
    o_own, residual, ox_send, ox_recv, b_send, b_recv, t_send, t_recv, f_send, f_recv, weight, result,
    *rest,
):
    n_pieces = len(PIECES)
    own, px_send, px_recv, rs_send, rs_recv, a_send, x = (
        rest[i * n_pieces:(i + 1) * n_pieces] for i in range(7))
    (l_sem, q_sem, o_sem, in_sem, rt_s, rt_r, ra_s, ra_r, px_s, px_r, rs_s, rs_r, a_s, a_r, h_s, h_r,
     ox_s, ox_r, b_s, b_r, t_s, t_r, f_s, f_r) = rest[7 * n_pieces:]
    r = lax.axis_index("dp")
    ep = lax.axis_index("ep")
    z = ep // 2
    c = ep % 2
    sib = z * 2 + 1 - c

    def remote(src, dst, ssem, rsem, dp_to, ep_to):
        return pltpu.make_async_remote_copy(
            src_ref=src, dst_ref=dst, send_sem=ssem, recv_sem=rsem,
            device_id=(dp_to, ep_to), device_id_type=MESH)

    def peer(dz):
        zz = lax.rem(z + dz, N_Z)
        return zz, zz * 2 + c

    barrier = pltpu.get_barrier_semaphore()

    def greet(i, carry):
        pl.semaphore_signal(barrier, inc=1, device_id=(lax.rem(r + i, N_DP), ep), device_id_type=MESH)
        return carry

    lax.fori_loop(1, N_DP, greet, 0)
    pl.semaphore_signal(barrier, inc=1, device_id=(r, sib), device_id_type=MESH)
    for dz in (1, 2, 3):
        pl.semaphore_signal(barrier, inc=1, device_id=(r, peer(dz)[1]), device_id_type=MESH)

    loads = [
        (lat_h, lat), (kr_h, kr), (vu_h, vu), (op_h, op), (routes_h, rt.at[z]),
        (gain_h, gain), (router_h, router), (gu_h.at[0], gu), (dn_h.at[0], dn), (lengths_h, lengths_s), (plan_h, plan_s),
    ]
    load = [pltpu.make_async_copy(s, d, l_sem.at[i]) for i, (s, d) in enumerate(loads)]
    qload = []
    for b in range(8):
        to = (b % 2) * HALF + (b // 2) * SPAN
        qload.append(pltpu.make_async_copy(
            qc_h.at[pl.ds(b * SPAN, SPAN)], qc.at[pl.ds(to, SPAN)], q_sem.at[b]))
        qload.append(pltpu.make_async_copy(
            qr_h.at[pl.ds(b * SPAN, SPAN)], qr.at[pl.ds(to, SPAN)], q_sem.at[8 + b]))
    for i in (9, 10, 4):
        load[i].start()
    load[0].start()
    load[1].start()
    for cp in qload:
        cp.start()
    load[2].start()

    load[0].wait()
    load[1].wait()
    for cp in qload:
        cp.wait()
    for i in (3, 5, 6, 7, 8):
        load[i].start()
    load[9].wait()
    length = lengths_s[r]
    latv = lat[...]
    krv = kr[...]
    place = lax.broadcasted_iota(jnp.int32, (S, S), 0)
    position = ((place % HALF) // SPAN * 2 + place // HALF) * SPAN + place % SPAN
    load[2].wait()
    for h in range(HEADS_HERE):
        att = attend(
            qc[:, h * LAT:(h + 1) * LAT], qr[:, h * ROPE:(h + 1) * ROPE], latv, krv, position, length)
        vals[:, h * VDIM:(h + 1) * VDIM] = mm(att, vu[h]).astype(BF)

    pl.semaphore_wait(barrier, N_DP - 1 + 1 + 3)
    for dz in (1, 2, 3):
        pl.semaphore_signal(in_sem, inc=1, device_id=(r, peer(dz)[1]), device_id_type=MESH)

    load[4].wait()
    load[10].wait()

    def rt_copy(dz, slot):
        return remote(rt.at[slot], rt.at[slot], rt_s.at[dz], rt_r.at[slot], r, peer(dz)[1])

    for dz in (1, 2, 3):
        rt_copy(dz, z).start()

    load[3].wait()
    order = (2, 1, 3, 0)

    def px_copy(p, zz):
        return remote(px_send[p].at[zz], px_recv[p].at[zz], px_s.at[p, zz], px_r.at[p, zz], r, sib)

    def rs_copy(p, dz):
        zz, to = peer(dz)
        return remote(rs_send[p].at[zz], rs_recv[p].at[z], rs_s.at[p, dz], rs_r.at[p, z], r, to)

    def pair_sum(p, dz):
        zz, _ = peer(dz)
        px_copy(p, zz).wait_recv()
        total = own[p][zz] + px_recv[p][zz].astype(F32)
        if dz:
            rs_send[p][zz] = total.astype(BF)
            rs_copy(p, dz).start()
        else:
            own[p][zz] = total

    def ra_all():
        part = rt_all.at[pl.ds(0, N_DP - 1)]
        return remote(part, part, ra_s.at[0], ra_r.at[0], r, sib)

    def spread_routes():
        for dz in (1, 2, 3):
            rt_copy(dz, peer(dz)[0]).wait_recv()

        @pl.when(c == 1)
        def _():
            rt_all[r] = rt[N_Z - 1]

            def ra_start(i, carry):
                to = lax.rem(r + i, N_DP)
                remote(rt_all.at[r], rt_all.at[r], ra_s.at[0], ra_r.at[0], to, ep).start()
                return carry

            lax.fori_loop(1, N_DP, ra_start, 0)

    valv = vals[...]
    steps = [(p, dz) for p in range(n_pieces) for dz in order]
    for n, (p, dz) in enumerate(steps):
        zz, _ = peer(dz)
        first, width = PIECES[p]
        block = mm(valv, op[:, pl.ds(pl.multiple_of(zz * COLS + first, 128), width)])
        top, bottom = block[:HALF], block[HALF:]
        own[p][zz] = jnp.where(c == 0, top, bottom)
        px_send[p][zz] = jnp.where(c == 0, bottom, top).astype(BF)
        px_copy(p, zz).start()
        if n >= LAG:
            pair_sum(*steps[n - LAG])
        if n == 4:
            spread_routes()
    for step in steps[len(steps) - LAG:]:
        pair_sum(*step)

    @pl.when(c == 1)
    def _():
        ra_all().wait_recv()
        rt_last[...] = rt_all[plan_s[r]]

    @pl.when(c == 0)
    def _():
        rt_last[...] = rt[N_Z - 1]

    slot = lax.broadcasted_iota(jnp.int32, (N_DP * SLOTS, HALF), 0)
    row = lax.broadcasted_iota(jnp.int32, (N_DP * SLOTS, HALF), 1)
    expert = slot // SLOTS
    t_row = lax.broadcasted_iota(jnp.int32, (HALF, HALF), 0)
    t_col = lax.broadcasted_iota(jnp.int32, (HALF, HALF), 1)
    earlier = jnp.where((t_row // SPAN == t_col // SPAN) & (t_row < t_col), 1.0, 0.0).astype(BF)
    same = (slot // 2) % N_Z == row // SPAN

    def slot_matrix(final):
        blocks = [rt[i] for i in range(N_Z - 1)] + [final]
        first = jnp.concatenate([block[0:1, :] for block in blocks], axis=1)
        second = jnp.concatenate([block[1:2, :] for block in blocks], axis=1)
        named = jnp.where((first == expert) | (second == expert), 1.0, 0.0)
        before = mm(named.astype(BF), earlier)
        return jnp.where(same & (before == (slot % 2).astype(F32)), named, 0.0)

    slots_t = slot_matrix(rt_last[...]).astype(BF)

    def a_copy(p, to, dz):
        return remote(
            a_send[p].at[to], x[p].at[z, c, r], a_s.at[p, dz], a_r.at[p, z], to, peer(dz)[1])

    for p, (first, width) in enumerate(PIECES):
        total = own[p][z]
        for dz in (1, 3, 2):
            zz, to = peer(dz)
            remote(rs_send[p].at[zz], rs_recv[p].at[zz], rs_s.at[p, dz], rs_r.at[p, zz], r, to).wait_recv()
            total = total + rs_recv[p][zz].astype(F32)
        a_send[p][...] = mm(slots_t, total.astype(BF)).reshape(N_DP, SLOTS, width).astype(BF)
        if p == 0:
            pl.semaphore_wait(in_sem, 3)

        def a_start(i, carry):
            to = lax.rem(r + i, N_DP)
            for dz in range(N_Z):
                a_copy(p, to, dz).start()
            return carry

        for dz in (1, 2, 3):
            a_copy(p, r, dz).start()
        lax.fori_loop(1, N_DP, a_start, 0)
        x[p][z, c, r] = a_send[p][r]

    slots = slot_matrix(rt[N_Z - 1]).T.astype(BF)

    half = N_DP * SLOTS
    to_row = lax.broadcasted_iota(jnp.int32, (2 * half, 2 * half), 0)
    from_row = lax.broadcasted_iota(jnp.int32, (2 * half, 2 * half), 1)
    rank = (to_row % half) // SLOTS
    partner = jnp.zeros_like(rank)
    for i in range(N_DP):
        partner = jnp.where(rank == i, plan_s[i], partner)
    moves = (to_row >= half) & (to_row % SLOTS >= SLOTS - 2)
    wanted = to_row + jnp.where(moves, (partner - rank) * SLOTS, 0)
    swap[...] = jnp.where(from_row == wanted, 1.0, 0.0).astype(BF)

    def a_wait(p, zz, count):
        part = x[p].at[zz, c, pl.ds(0, count)]
        remote(part, part, a_s.at[p, 0], a_r.at[p, zz], r, sib).wait_recv()

    def h_copy(p, zz, cc):
        return remote(x[p].at[zz, cc], x[p].at[zz, cc], h_s.at[p, zz], h_r.at[p, zz], r, sib)

    for i in (5, 6, 7, 8):
        load[i].wait()
    square[...] = jnp.zeros_like(square)
    gate[...] = jnp.zeros_like(gate)
    upper[...] = jnp.zeros_like(upper)
    logit[...] = jnp.zeros_like(logit)

    def expert_chunk(p, zz):
        first, width = PIECES[p]
        h_copy(p, zz, 1 - c).wait_recv()
        at = pl.multiple_of(zz * COLS + first, 128)
        m = x[p][zz].astype(F32).reshape(2 * half, width)
        square[...] += jnp.sum(m * m, axis=1, keepdims=True)
        xin = (m * gain[pl.ds(at, width)].reshape(1, width)).astype(BF)
        gate[...] += mm(xin, gu[0, pl.ds(at, width)])
        upper[...] += mm(xin, gu[1, pl.ds(at, width)])
        logit[...] += lax.dot_general(
            xin, router[:, pl.ds(at, width)], (((1,), (1,)), ((), ())), preferred_element_type=F32)

    previous = None
    for p in range(n_pieces):
        for dz in (0, 1, 3, 2):
            zz, _ = peer(dz)
            a_wait(p, zz, N_DP if dz else N_DP - 1)
            h_copy(p, zz, c).start()
            if previous is not None:
                expert_chunk(*previous)
            previous = (p, zz)
    expert_chunk(*previous)

    scale = lax.rsqrt(square[...] * (1.0 / D) + norm_eps)
    pick = lax.broadcasted_iota(jnp.int32, logit.shape, 1) == r
    chosen = jax.nn.sigmoid(jnp.sum(jnp.where(pick, logit[...], 0.0), axis=1, keepdims=True) * scale)
    swapv = swap[...]
    hidv = (jax.nn.silu(gate[...] * scale) * (upper[...] * scale) * chosen).astype(BF)
    hidv = mm(swapv, hidv).astype(BF)

    def ox_copy(zz):
        return remote(ox_send.at[zz], ox_recv.at[zz], ox_s.at[zz], ox_r.at[zz], r, sib)

    def out_sum(dz):
        zz, _ = peer(dz)
        ox_copy(zz).wait_recv()
        total = o_own[zz] + ox_recv[zz].astype(F32)
        if dz == 0:
            total = total + residual[...]
        b_send[zz] = total.reshape(N_DP, SLOTS, COLS).astype(BF)

        def b_start(i, carry):
            to = lax.rem(r + i, N_DP)
            remote(b_send.at[zz, to], b_recv.at[zz, r], b_s.at[zz], b_r.at[zz], to, ep).start()
            return carry

        lax.fori_loop(1, N_DP, b_start, 0)
        b_recv[zz, r] = b_send[zz, r]

    def t_start(i, carry):
        to = lax.rem(r + i, N_DP)
        remote(t_send.at[to], t_recv.at[r], t_s.at[0], t_r.at[0], to, ep).start()
        return carry

    for n, dz in enumerate(order):
        zz, _ = peer(dz)
        block = mm(hidv, dn[:, pl.ds(pl.multiple_of(zz * COLS, 128), COLS)])
        top, bottom = block[:half], block[half:]
        ox_send[zz] = jnp.where(c == 0, bottom, top).astype(BF)
        ox_copy(zz).start()
        o_own[zz] = jnp.where(c == 0, top, bottom)
        if n:
            out_sum(order[n - 1])
        if n == 1:
            column = lax.broadcasted_iota(jnp.int32, (2 * half, EXTRA), 1)
            high = chosen.astype(BF).astype(F32)
            tail = jnp.where(column == 0, high, jnp.where(column == 1, chosen - high, 0.0)).astype(BF)
            tail = mm(swapv, tail)
            chosen = tail[:, 0:1] + tail[:, 1:2]
            t_send[...] = jnp.where(c == 0, tail[:half], tail[half:]).reshape(N_DP, SLOTS, EXTRA).astype(BF)
            lax.fori_loop(1, N_DP, t_start, 0)
            t_recv[r] = t_send[r]
        if n == 2:
            swap_half = jnp.where(c == 0, swapv[:half, :half], swapv[half:, half:])
            mine = jnp.where(c == 0, chosen[:half], chosen[half:]) * (1.0 / route_scale)
            for p, (first, width) in enumerate(PIECES):
                rows_in = x[p][z, c].astype(F32).reshape(half, width).astype(BF)
                residual[:, first:first + width] = mm(swap_half, rows_in) * mine
    out_sum(order[-1])

    def f_copy(dz, zz):
        to_z, to = peer(dz)
        return remote(
            f_send.at[zz, to_z], f_recv.at[z, zz], f_s.at[zz, dz], f_r.at[z, zz], r, to)

    def b_all(zz):
        part = b_recv.at[zz, pl.ds(0, N_DP - 1)]
        return remote(part, part, b_s.at[zz], b_r.at[zz], r, sib)

    for dz in order:
        zz, _ = peer(dz)
        b_all(zz).wait_recv()
        joined = mm(slots, b_recv[zz].astype(F32).reshape(half, COLS).astype(BF))
        f_send[zz] = joined.reshape(N_Z, SPAN, COLS).astype(BF)
        for to in (2, 1, 3):
            f_copy(to, zz).start()
    t_part = t_recv.at[pl.ds(0, N_DP - 1)]
    remote(t_part, t_part, t_s.at[0], t_r.at[0], r, sib).wait_recv()
    weight[...] = mm(slots, t_recv[...].astype(F32).reshape(half, EXTRA).astype(BF)).reshape(
        N_Z, SPAN, EXTRA)
    mine = weight[z]
    factor = route_scale / (mine[:, 0:1] + mine[:, 1:2])

    def store(zz):
        columns = pl.ds(pl.multiple_of(zz * COLS, 128), COLS)
        return pltpu.make_async_copy(result.at[zz], out.at[:, columns], o_sem.at[zz])

    for dz in order:
        zz, _ = peer(dz)
        total = f_send[zz, z].astype(F32)
        for frm in (1, 3, 2):
            from_z, _ = peer(frm)
            remote(
                f_send.at[zz, z], f_recv.at[from_z, zz], f_s.at[zz, frm], f_r.at[from_z, zz], r, sib
            ).wait_recv()
            total = total + f_recv[from_z, zz].astype(F32)
        result[zz] = (total * factor).astype(BF)
        store(zz).start()

    for i in range(N_Z):
        store(i).wait()
    for dz in range(N_Z):
        zz, to = peer(dz)
        count = N_DP if dz else N_DP - 1
        b_all(zz).wait_send()
        for p in range(n_pieces):
            part = a_send[p].at[pl.ds(0, count)]
            remote(part, part, a_s.at[p, dz], a_r.at[p, zz], r, sib).wait_send()
            px_copy(p, zz).wait_send()
            h_copy(p, zz, c).wait_send()
            if dz:
                rs_copy(p, dz).wait_send()
        ox_copy(zz).wait_send()
        if dz:
            rt_copy(dz, z).wait_send()
            for chunk in range(N_Z):
                f_copy(dz, chunk).wait_send()
    remote(t_part, t_part, t_s.at[0], t_r.at[0], r, sib).wait_send()

    @pl.when(c == 1)
    def _():
        ra_all().wait_send()


def per_device(
    queries_c, queries_r, latents, key_rope, value_up, out_proj, norm_gain, router, gate_up, down,
    routes, lengths, plan,
):
    any_spec = pl.BlockSpec(memory_space=pl.ANY)
    vm = pltpu.VMEM
    dma = pltpu.SemaphoreType.DMA
    half = N_DP * SLOTS
    scratch = [
        pltpu.SMEM((N_DP,), jnp.int32), pltpu.SMEM((N_DP,), jnp.int32),
        vm((S, HEADS_HERE * LAT), BF), vm((S, HEADS_HERE * ROPE), BF), vm((S, LAT), BF), vm((ROPE, S), BF),
        vm((HEADS_HERE, LAT, VDIM), BF), vm((HEADS_HERE * VDIM, D), BF), vm((D,), F32),
        vm((N_DP, D), BF), vm((2, D, 256), BF), vm((256, D), BF),
        vm((N_Z, 2, SPAN), jnp.int32), vm((N_DP, 2, SPAN), jnp.int32), vm((2, SPAN), jnp.int32),
        vm((S, HEADS_HERE * VDIM), BF),
        vm((2 * half, 256), F32), vm((2 * half, 256), F32), vm((2 * half, N_DP), F32), vm((2 * half, 1), F32),
        vm((2 * half, 2 * half), BF),
        vm((N_Z, half, COLS), F32), vm((half, COLS), F32), vm((N_Z, half, COLS), BF), vm((N_Z, half, COLS), BF),
        vm((N_Z, N_DP, SLOTS, COLS), BF), vm((N_Z, N_DP, SLOTS, COLS), BF),
        vm((N_DP, SLOTS, EXTRA), BF), vm((N_DP, SLOTS, EXTRA), BF),
        vm((N_Z, N_Z, SPAN, COLS), BF), vm((N_Z, N_Z, SPAN, COLS), BF),
        vm((N_Z, SPAN, EXTRA), F32), vm((N_Z, SPAN, COLS), BF),
    ]
    widths = [width for _, width in PIECES]
    n_pieces = len(PIECES)
    scratch += [vm((N_Z, HALF, w), F32) for w in widths]
    for _ in range(4):
        scratch += [vm((N_Z, HALF, w), BF) for w in widths]
    scratch += [vm((N_DP, SLOTS, w), BF) for w in widths]
    scratch += [vm((N_Z, 2, N_DP, SLOTS, w), BF) for w in widths]
    by_piece = dma((n_pieces, 4))
    scratch += [
        dma((11,)), dma((16,)), dma((4,)), pltpu.SemaphoreType.REGULAR, dma((4,)), dma((4,)), dma((1,)), dma((1,)),
        by_piece, by_piece, by_piece, by_piece, by_piece, by_piece, by_piece, by_piece,
        dma((4,)), dma((4,)), dma((4,)), dma((4,)), dma((1,)), dma((1,)), dma((4, 4)), dma((4, 4)),
    ]
    return pl.pallas_call(
        kernel,
        out_shape=jax.ShapeDtypeStruct((SPAN, D), BF),
        in_specs=[any_spec] * 13,
        out_specs=any_spec,
        scratch_shapes=scratch,
        compiler_params=pltpu.CompilerParams(
            collective_id=0, has_side_effects=True, vmem_limit_bytes=56 * 1024 * 1024),
        cost_estimate=pl.CostEstimate(flops=3 * 10**9, bytes_accessed=16 * 10**6, transcendentals=10**6),
    )(
        lengths, plan, queries_c, queries_r, latents, key_rope, value_up, out_proj,
        norm_gain, router.T, gate_up, down, routes.T,
    )


def solution(mesh):
    placed = (
        P("dp", "ep"),
        P("dp", "ep"),
        P("dp", None),
        P(None, "dp"),
        P("ep", None, None),
        P("ep", None),
        P(),
        P(),
        P("dp", None, None, "ep"),
        P("dp", "ep", None),
        P(("dp", "ep"), None),
        P(),
        P(),
    )
    return jax.shard_map(
        per_device, mesh=mesh, in_specs=placed, out_specs=P(("dp", "ep"), None), check_vma=False
    )
```

```python
import jax
import jax.numpy as jnp
from jax import lax
from jax.experimental import pallas as pl
from jax.experimental.pallas import tpu as pltpu
from jax.sharding import PartitionSpec as P

MESH = pl.DeviceIdType.MESH
BF = jnp.bfloat16
F32 = jnp.float32

D = 3584
LAT = 512
ROPE = 64
VDIM = 128
S = 128
SPAN = 16
HEADS_HERE = 8
N_DP = 16
N_Z = 4
HALF = 64
COLS = D // N_Z
SLOTS = 8
EXTRA = 128
BACK = ((0, 384), (384, 512))
LAG = 2
PIECES = ((0, 384), (384, 512))

softmax_scale = 192.0 ** (-0.5)
route_scale = 2.5
norm_eps = 1e-06


def mm(a, b):
    return jnp.dot(a, b, preferred_element_type=F32)


def attend(q, qr, lat, kr, position, length):
    scores = lax.dot_general(q, lat, (((1,), (1,)), ((), ())), preferred_element_type=F32)
    scores = (scores + mm(qr, kr)) * softmax_scale
    key = lax.broadcasted_iota(jnp.int32, scores.shape, 1)
    visible = (key <= position) & (key < length)
    highest = jnp.max(jnp.where(visible, scores, -jnp.inf), axis=1, keepdims=True)
    weights = jnp.where(visible, jnp.exp(scores - highest), 0.0)
    totals = jnp.sum(weights, axis=1, keepdims=True)
    mixed = mm(weights.astype(BF), lat) / totals
    return jnp.where(position[:, :1] < length, mixed, 0.0).astype(BF)


def kernel(
    lengths_h, plan_h, qc_h, qr_h, lat_h, kr_h, vu_h, op_h, gain_h, router_h, gu_h, dn_h, routes_h,
    out,
    lengths_s, plan_s, qc, qr, lat, kr, vu, op, gain, router, gu, dn, rt, rt_all, rt_last,
    vals, gate, upper, logit, square, swap,
    residual, c_send, c_recv, d_send, d_recv, e_send, e_recv, b_send, b_recv, t_send, t_recv,
    f_send, f_recv, weight, result,
    *rest,
):
    n_pieces = len(PIECES)
    own, px_send, px_recv, rs_send, rs_recv, a_send, x, o_own, ox_send, ox_recv = (
        rest[i * n_pieces:(i + 1) * n_pieces] for i in range(10))
    (l_sem, q_sem, o_sem, in_sem, rt_s, rt_r, ra_s, ra_r, px_s, px_r, rs_s, rs_r, a_s, a_r, h_s, h_r,
     ox_s, ox_r, b_s, b_r, t_s, t_r, f_s, f_r, c_s, c_r, d_s, d_r, e_s, e_r) = rest[10 * n_pieces:]
    r = lax.axis_index("dp")
    ep = lax.axis_index("ep")
    z = ep // 2
    c = ep % 2
    sib = z * 2 + 1 - c

    def remote(src, dst, ssem, rsem, dp_to, ep_to):
        return pltpu.make_async_remote_copy(
            src_ref=src, dst_ref=dst, send_sem=ssem, recv_sem=rsem,
            device_id=(dp_to, ep_to), device_id_type=MESH)

    def peer(dz):
        zz = lax.rem(z + dz, N_Z)
        return zz, zz * 2 + c

    def other(i):
        return lax.rem(r + N_DP * N_DP + (1 - 2 * c) * i, N_DP)

    barrier = pltpu.get_barrier_semaphore()

    def greet(i, carry):
        pl.semaphore_signal(barrier, inc=1, device_id=(lax.rem(r + i, N_DP), ep), device_id_type=MESH)
        return carry

    lax.fori_loop(1, N_DP, greet, 0)
    pl.semaphore_signal(barrier, inc=1, device_id=(r, sib), device_id_type=MESH)
    for dz in (1, 2, 3):
        pl.semaphore_signal(barrier, inc=1, device_id=(r, peer(dz)[1]), device_id_type=MESH)

    loads = [
        (lat_h, lat), (kr_h, kr), (vu_h, vu), (op_h, op), (routes_h, rt.at[z]),
        (gain_h, gain), (router_h, router), (gu_h.at[0], gu), (dn_h.at[0], dn), (lengths_h, lengths_s), (plan_h, plan_s),
    ]
    load = [pltpu.make_async_copy(s, d, l_sem.at[i]) for i, (s, d) in enumerate(loads)]
    qload = []
    for b in range(8):
        to = (b % 2) * HALF + (b // 2) * SPAN
        qload.append(pltpu.make_async_copy(
            qc_h.at[pl.ds(b * SPAN, SPAN)], qc.at[pl.ds(to, SPAN)], q_sem.at[b]))
        qload.append(pltpu.make_async_copy(
            qr_h.at[pl.ds(b * SPAN, SPAN)], qr.at[pl.ds(to, SPAN)], q_sem.at[8 + b]))
    for i in (9, 10, 4):
        load[i].start()
    load[0].start()
    load[1].start()
    for cp in qload:
        cp.start()
    load[2].start()

    load[0].wait()
    load[1].wait()
    for cp in qload:
        cp.wait()
    for i in (3, 5, 6, 7, 8):
        load[i].start()
    load[9].wait()
    length = lengths_s[r]
    latv = lat[...]
    krv = kr[...]
    place = lax.broadcasted_iota(jnp.int32, (S, S), 0)
    position = ((place % HALF) // SPAN * 2 + place // HALF) * SPAN + place % SPAN
    load[2].wait()
    for h in range(HEADS_HERE):
        att = attend(
            qc[:, h * LAT:(h + 1) * LAT], qr[:, h * ROPE:(h + 1) * ROPE], latv, krv, position, length)
        vals[:, h * VDIM:(h + 1) * VDIM] = mm(att, vu[h]).astype(BF)

    pl.semaphore_wait(barrier, N_DP - 1 + 1 + 3)
    for dz in (1, 2, 3):
        pl.semaphore_signal(in_sem, inc=1, device_id=(r, peer(dz)[1]), device_id_type=MESH)

    load[4].wait()
    load[10].wait()

    def rt_copy(dz, slot):
        return remote(rt.at[slot], rt.at[slot], rt_s.at[dz], rt_r.at[slot], r, peer(dz)[1])

    for dz in (1, 2, 3):
        rt_copy(dz, z).start()

    load[3].wait()
    order = (2, 1, 3, 0)

    def px_copy(p, zz):
        return remote(px_send[p].at[zz], px_recv[p].at[zz], px_s.at[p, zz], px_r.at[p, zz], r, sib)

    def rs_copy(p, dz):
        zz, to = peer(dz)
        return remote(rs_send[p].at[zz], rs_recv[p].at[z], rs_s.at[p, dz], rs_r.at[p, z], r, to)

    def pair_sum(p, dz):
        zz, _ = peer(dz)
        px_copy(p, zz).wait_recv()
        total = own[p][zz] + px_recv[p][zz].astype(F32)
        if dz:
            rs_send[p][zz] = total.astype(BF)
            rs_copy(p, dz).start()
        else:
            own[p][zz] = total

    def ra_all():
        part = rt_all.at[pl.ds(0, N_DP - 1)]
        return remote(part, part, ra_s.at[0], ra_r.at[0], r, sib)

    def spread_routes():
        for dz in (1, 2, 3):
            rt_copy(dz, peer(dz)[0]).wait_recv()

        @pl.when(c == 1)
        def _():
            rt_all[r] = rt[N_Z - 1]

            def ra_start(i, carry):
                to = other(i)
                remote(rt_all.at[r], rt_all.at[r], ra_s.at[0], ra_r.at[0], to, ep).start()
                return carry

            lax.fori_loop(1, N_DP, ra_start, 0)

    valv = vals[...]
    steps = [(p, dz) for p in range(n_pieces) for dz in order]
    for n, (p, dz) in enumerate(steps):
        zz, _ = peer(dz)
        first, width = PIECES[p]
        block = mm(valv, op[:, pl.ds(pl.multiple_of(zz * COLS + first, 128), width)])
        top, bottom = block[:HALF], block[HALF:]
        own[p][zz] = jnp.where(c == 0, top, bottom)
        px_send[p][zz] = jnp.where(c == 0, bottom, top).astype(BF)
        px_copy(p, zz).start()
        if n >= LAG:
            pair_sum(*steps[n - LAG])
        if n == 4:
            spread_routes()
    for step in steps[len(steps) - LAG:]:
        pair_sum(*step)

    @pl.when(c == 1)
    def _():
        ra_all().wait_recv()
        rt_last[...] = rt_all[plan_s[r]]

    @pl.when(c == 0)
    def _():
        rt_last[...] = rt[N_Z - 1]

    slot = lax.broadcasted_iota(jnp.int32, (N_DP * SLOTS, HALF), 0)
    row = lax.broadcasted_iota(jnp.int32, (N_DP * SLOTS, HALF), 1)
    expert = slot // SLOTS
    t_row = lax.broadcasted_iota(jnp.int32, (HALF, HALF), 0)
    t_col = lax.broadcasted_iota(jnp.int32, (HALF, HALF), 1)
    earlier = jnp.where((t_row // SPAN == t_col // SPAN) & (t_row < t_col), 1.0, 0.0).astype(BF)
    same = (slot // 2) % N_Z == row // SPAN

    def slot_matrix(final):
        blocks = [rt[i] for i in range(N_Z - 1)] + [final]
        first = jnp.concatenate([block[0:1, :] for block in blocks], axis=1)
        second = jnp.concatenate([block[1:2, :] for block in blocks], axis=1)
        named = jnp.where((first == expert) | (second == expert), 1.0, 0.0)
        before = mm(named.astype(BF), earlier)
        return jnp.where(same & (before == (slot % 2).astype(F32)), named, 0.0)

    slots_t = slot_matrix(rt_last[...]).astype(BF)

    def a_copy(p, to, dz):
        return remote(
            a_send[p].at[to], x[p].at[z, c, r], a_s.at[p, dz], a_r.at[p, z], to, peer(dz)[1])

    for p, (first, width) in enumerate(PIECES):
        total = own[p][z]
        for dz in (1, 3, 2):
            zz, to = peer(dz)
            remote(rs_send[p].at[zz], rs_recv[p].at[zz], rs_s.at[p, dz], rs_r.at[p, zz], r, to).wait_recv()
            total = total + rs_recv[p][zz].astype(F32)
        a_send[p][...] = mm(slots_t, total.astype(BF)).reshape(N_DP, SLOTS, width).astype(BF)
        if p == 0:
            pl.semaphore_wait(in_sem, 3)

        def a_start(i, carry):
            to = other(i)
            for dz in range(N_Z):
                a_copy(p, to, dz).start()
            return carry

        for dz in (1, 2, 3):
            a_copy(p, r, dz).start()
        lax.fori_loop(1, N_DP, a_start, 0)
        x[p][z, c, r] = a_send[p][r]

    slots = slot_matrix(rt[N_Z - 1]).T.astype(BF)

    half = N_DP * SLOTS
    to_row = lax.broadcasted_iota(jnp.int32, (2 * half, 2 * half), 0)
    from_row = lax.broadcasted_iota(jnp.int32, (2 * half, 2 * half), 1)
    rank = (to_row % half) // SLOTS
    partner = jnp.zeros_like(rank)
    for i in range(N_DP):
        partner = jnp.where(rank == i, plan_s[i], partner)
    moves = (to_row >= half) & (to_row % SLOTS >= SLOTS - 2)
    wanted = to_row + jnp.where(moves, (partner - rank) * SLOTS, 0)
    swap[...] = jnp.where(from_row == wanted, 1.0, 0.0).astype(BF)

    def a_wait(p, zz, count):
        part = x[p].at[zz, c, pl.ds(0, count)]
        remote(part, part, a_s.at[p, 0], a_r.at[p, zz], r, sib).wait_recv()

    def h_copy(p, zz, cc):
        return remote(x[p].at[zz, cc], x[p].at[zz, cc], h_s.at[p, zz], h_r.at[p, zz], r, sib)

    for i in (5, 6, 7, 8):
        load[i].wait()
    square[...] = jnp.zeros_like(square)
    gate[...] = jnp.zeros_like(gate)
    upper[...] = jnp.zeros_like(upper)
    logit[...] = jnp.zeros_like(logit)

    def expert_chunk(p, zz):
        first, width = PIECES[p]
        h_copy(p, zz, 1 - c).wait_recv()
        at = pl.multiple_of(zz * COLS + first, 128)
        m = x[p][zz].astype(F32).reshape(2 * half, width)
        square[...] += jnp.sum(m * m, axis=1, keepdims=True)
        xin = (m * gain[pl.ds(at, width)].reshape(1, width)).astype(BF)
        gate[...] += mm(xin, gu[0, pl.ds(at, width)])
        upper[...] += mm(xin, gu[1, pl.ds(at, width)])
        logit[...] += lax.dot_general(
            xin, router[:, pl.ds(at, width)], (((1,), (1,)), ((), ())), preferred_element_type=F32)

    previous = None
    for p in range(n_pieces):
        for dz in (0, 1, 3, 2):
            zz, _ = peer(dz)
            a_wait(p, zz, N_DP if dz else N_DP - 1)
            h_copy(p, zz, c).start()
            if previous is not None:
                expert_chunk(*previous)
            previous = (p, zz)
    expert_chunk(*previous)

    scale = lax.rsqrt(square[...] * (1.0 / D) + norm_eps)
    pick = lax.broadcasted_iota(jnp.int32, logit.shape, 1) == r
    chosen = jax.nn.sigmoid(jnp.sum(jnp.where(pick, logit[...], 0.0), axis=1, keepdims=True) * scale)
    swapv = swap[...]
    hidv = (jax.nn.silu(gate[...] * scale) * (upper[...] * scale) * chosen).astype(BF)
    hidv = mm(swapv, hidv).astype(BF)

    def ox_copy(p, zz):
        return remote(ox_send[p].at[zz], ox_recv[p].at[zz], ox_s.at[p, zz], ox_r.at[p, zz], r, sib)

    def c_copy(dz):
        zz, to = peer(dz)
        return remote(c_send.at[zz], c_recv.at[z], c_s.at[dz], c_r.at[z], r, to)

    def b_copy(zz, to):
        return remote(b_send.at[zz, to], b_recv.at[zz, r], b_s.at[zz], b_r.at[zz], to, ep)

    def b_all(zz):
        part = b_recv.at[zz, pl.ds(0, N_DP - 1)]
        return remote(part, part, b_s.at[zz], b_r.at[zz], r, sib)

    def d_copy(to):
        return remote(d_send.at[to], d_recv.at[r], d_s.at[0], d_r.at[0], to, ep)

    def d_all():
        part = d_recv.at[pl.ds(0, N_DP - 1)]
        return remote(part, part, d_s.at[0], d_r.at[0], r, sib)

    def to_ranks(make):
        def start(i, carry):
            make(other(i)).start()
            return carry

        lax.fori_loop(1, N_DP, start, 0)

    def out_sum(p, dz):
        zz, _ = peer(dz)
        first, width = BACK[p]
        ox_copy(p, zz).wait_recv()
        total = o_own[p][zz] + ox_recv[p][zz].astype(F32)
        if dz == 0:
            total = total + residual[:, first:first + width]
        if p == 1:
            b_send[zz] = total.reshape(N_DP, SLOTS, width).astype(BF)
            to_ranks(lambda to: b_copy(zz, to))
            b_recv[zz, r] = b_send[zz, r]
        elif dz:
            c_send[zz] = total.astype(BF)
            c_copy(dz).start()
        else:
            o_own[p][zz] = total

    for n, (p, dz) in enumerate(steps):
        zz, _ = peer(dz)
        first, width = BACK[p]
        block = mm(hidv, dn[:, pl.ds(pl.multiple_of(zz * COLS + first, 128), width)])
        top, bottom = block[:half], block[half:]
        ox_send[p][zz] = jnp.where(c == 0, bottom, top).astype(BF)
        ox_copy(p, zz).start()
        o_own[p][zz] = jnp.where(c == 0, top, bottom)
        if n == 3:
            column = lax.broadcasted_iota(jnp.int32, (2 * half, EXTRA), 1)
            high = chosen.astype(BF).astype(F32)
            tail = jnp.where(column == 0, high, jnp.where(column == 1, chosen - high, 0.0)).astype(BF)
            tail = mm(swapv, tail)
            chosen = tail[:, 0:1] + tail[:, 1:2]
            t_send[...] = jnp.where(c == 0, tail[:half], tail[half:]).reshape(N_DP, SLOTS, EXTRA).astype(BF)
            swap_half = jnp.where(c == 0, swapv[:half, :half], swapv[half:, half:])
            mine = jnp.where(c == 0, chosen[:half], chosen[half:]) * (1.0 / route_scale)
            for q, (start, size) in enumerate(PIECES):
                rows_in = x[q][z, c].astype(F32).reshape(half, size).astype(BF)
                residual[:, start:start + size] = mm(swap_half, rows_in) * mine
        if n >= 3:
            out_sum(*steps[n - 3])
    for step in steps[len(steps) - 3:]:
        out_sum(*step)

    total = o_own[0][z]
    for dz in (1, 3, 2):
        zz, to = peer(dz)
        remote(c_send.at[zz], c_recv.at[zz], c_s.at[dz], c_r.at[zz], r, to).wait_recv()
        total = total + c_recv[zz].astype(F32)
    d_send[...] = total.reshape(N_DP, SLOTS, BACK[0][1]).astype(BF)
    to_ranks(d_copy)
    d_recv[r] = d_send[r]

    def t_copy(to):
        return remote(t_send.at[to], t_recv.at[r], t_s.at[0], t_r.at[0], to, ep)

    to_ranks(t_copy)
    t_recv[r] = t_send[r]

    def f_copy(dz, zz):
        to_z, to = peer(dz)
        return remote(
            f_send.at[zz, to_z], f_recv.at[z, zz], f_s.at[zz, dz], f_r.at[z, zz], r, to)

    def e_copy(dz):
        to_z, to = peer(dz)
        return remote(e_send.at[to_z], e_recv.at[z], e_s.at[dz], e_r.at[z], r, to)

    for dz in order:
        zz, _ = peer(dz)
        b_all(zz).wait_recv()
        joined = mm(slots, b_recv[zz].astype(F32).reshape(half, BACK[1][1]).astype(BF))
        f_send[zz] = joined.reshape(N_Z, SPAN, BACK[1][1]).astype(BF)
        for to in (2, 1, 3):
            f_copy(to, zz).start()
    d_all().wait_recv()
    joined = mm(slots, d_recv[...].astype(F32).reshape(half, BACK[0][1]).astype(BF))
    e_send[...] = joined.reshape(N_Z, SPAN, BACK[0][1]).astype(BF)
    for dz in (2, 1, 3):
        e_copy(dz).start()
    e_recv[z] = e_send[z]
    t_part = t_recv.at[pl.ds(0, N_DP - 1)]
    remote(t_part, t_part, t_s.at[0], t_r.at[0], r, sib).wait_recv()
    weight[...] = mm(slots, t_recv[...].astype(F32).reshape(half, EXTRA).astype(BF)).reshape(
        N_Z, SPAN, EXTRA)
    mine = weight[z]
    factor = route_scale / (mine[:, 0:1] + mine[:, 1:2])

    def store(zz):
        columns = pl.ds(pl.multiple_of(zz * COLS, 128), COLS)
        return pltpu.make_async_copy(result.at[zz], out.at[:, columns], o_sem.at[zz])

    for dz in order:
        zz, _ = peer(dz)
        total = f_send[zz, z].astype(F32)
        for frm in (1, 3, 2):
            from_z, _ = peer(frm)
            remote(
                f_send.at[zz, z], f_recv.at[from_z, zz], f_s.at[zz, frm], f_r.at[from_z, zz], r, sib
            ).wait_recv()
            total = total + f_recv[from_z, zz].astype(F32)
        result[zz, :, BACK[1][0]:] = (total * factor).astype(BF)
    for dz in (0, 1, 3, 2):
        zz, to = peer(dz)
        if dz:
            remote(e_send.at[zz], e_recv.at[zz], e_s.at[dz], e_r.at[zz], r, to).wait_recv()
        result[zz, :, :BACK[1][0]] = (e_recv[zz].astype(F32) * factor).astype(BF)
        store(zz).start()

    for i in range(N_Z):
        store(i).wait()
    for dz in range(N_Z):
        zz, to = peer(dz)
        count = N_DP if dz else N_DP - 1
        b_all(zz).wait_send()
        for p in range(n_pieces):
            part = a_send[p].at[pl.ds(0, count)]
            remote(part, part, a_s.at[p, dz], a_r.at[p, zz], r, sib).wait_send()
            px_copy(p, zz).wait_send()
            ox_copy(p, zz).wait_send()
            h_copy(p, zz, c).wait_send()
            if dz:
                rs_copy(p, dz).wait_send()
        if dz:
            rt_copy(dz, z).wait_send()
            c_copy(dz).wait_send()
            e_copy(dz).wait_send()
            for chunk in range(N_Z):
                f_copy(dz, chunk).wait_send()
    remote(t_part, t_part, t_s.at[0], t_r.at[0], r, sib).wait_send()
    d_all().wait_send()

    @pl.when(c == 1)
    def _():
        ra_all().wait_send()


def per_device(
    queries_c, queries_r, latents, key_rope, value_up, out_proj, norm_gain, router, gate_up, down,
    routes, lengths, plan,
):
    any_spec = pl.BlockSpec(memory_space=pl.ANY)
    vm = pltpu.VMEM
    dma = pltpu.SemaphoreType.DMA
    half = N_DP * SLOTS
    scratch = [
        pltpu.SMEM((N_DP,), jnp.int32), pltpu.SMEM((N_DP,), jnp.int32),
        vm((S, HEADS_HERE * LAT), BF), vm((S, HEADS_HERE * ROPE), BF), vm((S, LAT), BF), vm((ROPE, S), BF),
        vm((HEADS_HERE, LAT, VDIM), BF), vm((HEADS_HERE * VDIM, D), BF), vm((D,), F32),
        vm((N_DP, D), BF), vm((2, D, 256), BF), vm((256, D), BF),
        vm((N_Z, 2, SPAN), jnp.int32), vm((N_DP, 2, SPAN), jnp.int32), vm((2, SPAN), jnp.int32),
        vm((S, HEADS_HERE * VDIM), BF),
        vm((2 * half, 256), F32), vm((2 * half, 256), F32), vm((2 * half, N_DP), F32), vm((2 * half, 1), F32),
        vm((2 * half, 2 * half), BF),
        vm((half, COLS), F32), vm((N_Z, half, BACK[0][1]), BF), vm((N_Z, half, BACK[0][1]), BF),
        vm((N_DP, SLOTS, BACK[0][1]), BF), vm((N_DP, SLOTS, BACK[0][1]), BF),
        vm((N_Z, SPAN, BACK[0][1]), BF), vm((N_Z, SPAN, BACK[0][1]), BF),
        vm((N_Z, N_DP, SLOTS, BACK[1][1]), BF), vm((N_Z, N_DP, SLOTS, BACK[1][1]), BF),
        vm((N_DP, SLOTS, EXTRA), BF), vm((N_DP, SLOTS, EXTRA), BF),
        vm((N_Z, N_Z, SPAN, BACK[1][1]), BF), vm((N_Z, N_Z, SPAN, BACK[1][1]), BF),
        vm((N_Z, SPAN, EXTRA), F32), vm((N_Z, SPAN, COLS), BF),
    ]
    widths = [width for _, width in PIECES]
    n_pieces = len(PIECES)
    scratch += [vm((N_Z, HALF, w), F32) for w in widths]
    for _ in range(4):
        scratch += [vm((N_Z, HALF, w), BF) for w in widths]
    scratch += [vm((N_DP, SLOTS, w), BF) for w in widths]
    scratch += [vm((N_Z, 2, N_DP, SLOTS, w), BF) for w in widths]
    backs = [width for _, width in BACK]
    scratch += [vm((N_Z, half, w), F32) for w in backs]
    for _ in range(2):
        scratch += [vm((N_Z, half, w), BF) for w in backs]
    by_piece = dma((n_pieces, 4))
    scratch += [
        dma((11,)), dma((16,)), dma((4,)), pltpu.SemaphoreType.REGULAR, dma((4,)), dma((4,)), dma((1,)), dma((1,)),
        by_piece, by_piece, by_piece, by_piece, by_piece, by_piece, by_piece, by_piece,
        by_piece, by_piece, dma((4,)), dma((4,)), dma((1,)), dma((1,)), dma((4, 4)), dma((4, 4)),
        dma((4,)), dma((4,)), dma((1,)), dma((1,)), dma((4,)), dma((4,)),
    ]
    return pl.pallas_call(
        kernel,
        out_shape=jax.ShapeDtypeStruct((SPAN, D), BF),
        in_specs=[any_spec] * 13,
        out_specs=any_spec,
        scratch_shapes=scratch,
        compiler_params=pltpu.CompilerParams(
            collective_id=0, has_side_effects=True, vmem_limit_bytes=56 * 1024 * 1024),
        cost_estimate=pl.CostEstimate(flops=3 * 10**9, bytes_accessed=16 * 10**6, transcendentals=10**6),
    )(
        lengths, plan, queries_c, queries_r, latents, key_rope, value_up, out_proj,
        norm_gain, router.T, gate_up, down, routes.T,
    )


def solution(mesh):
    placed = (
        P("dp", "ep"),
        P("dp", "ep"),
        P("dp", None),
        P(None, "dp"),
        P("ep", None, None),
        P("ep", None),
        P(),
        P(),
        P("dp", None, None, "ep"),
        P("dp", "ep", None),
        P(("dp", "ep"), None),
        P(),
        P(),
    )
    return jax.shard_map(
        per_device, mesh=mesh, in_specs=placed, out_specs=P(("dp", "ep"), None), check_vma=False
    )
```

```python
import jax
import jax.numpy as jnp
from jax import lax
from jax.experimental import pallas as pl
from jax.experimental.pallas import tpu as pltpu
from jax.sharding import PartitionSpec as P

MESH = pl.DeviceIdType.MESH
BF = jnp.bfloat16
F32 = jnp.float32

D = 3584
LAT = 512
ROPE = 64
VDIM = 128
S = 128
SPAN = 16
HEADS_HERE = 8
N_DP = 16
N_Z = 4
HALF = 64
COLS = D // N_Z
SLOTS = 8
EXTRA = 128
BACK = ((0, 384), (384, 512))
LAG = 2
PIECES = ((0, 384), (384, 512))

softmax_scale = 192.0 ** (-0.5)
route_scale = 2.5
norm_eps = 1e-06


def mm(a, b):
    return jnp.dot(a, b, preferred_element_type=F32)


def attend(q, qr, lat, kr, position, length):
    scores = lax.dot_general(q, lat, (((1,), (1,)), ((), ())), preferred_element_type=F32)
    scores = (scores + mm(qr, kr)) * softmax_scale
    key = lax.broadcasted_iota(jnp.int32, scores.shape, 1)
    visible = (key <= position) & (key < length)
    highest = jnp.max(jnp.where(visible, scores, -jnp.inf), axis=1, keepdims=True)
    weights = jnp.where(visible, jnp.exp(scores - highest), 0.0)
    totals = jnp.sum(weights, axis=1, keepdims=True)
    mixed = mm(weights.astype(BF), lat) / totals
    return jnp.where(position[:, :1] < length, mixed, 0.0).astype(BF)


def kernel(
    lengths_h, plan_h, qc_h, qr_h, lat_h, kr_h, vu_h, op_h, gain_h, router_h, gu_h, dn_h, routes_h,
    out,
    lengths_s, plan_s, qc, qr, lat, kr, vu, op, gain, router, gu, dn, rt, rt_all, rt_last,
    vals, gate, upper, logit, square, swap,
    residual, c_send, c_recv, d_send, d_recv, e_send, e_recv, b_send, b_recv, t_send, t_recv,
    f_send, f_recv, weight, result,
    *rest,
):
    n_pieces = len(PIECES)
    own, px_send, px_recv, rs_send, rs_recv, a_send, x, o_own, ox_send, ox_recv = (
        rest[i * n_pieces:(i + 1) * n_pieces] for i in range(10))
    (l_sem, q_sem, o_sem, in_sem, rt_s, rt_r, ra_s, ra_r, px_s, px_r, rs_s, rs_r, a_s, a_r, h_s, h_r,
     ox_s, ox_r, b_s, b_r, t_s, t_r, f_s, f_r, c_s, c_r, d_s, d_r, e_s, e_r) = rest[10 * n_pieces:]
    r = lax.axis_index("dp")
    ep = lax.axis_index("ep")
    z = ep // 2
    c = ep % 2
    sib = z * 2 + 1 - c

    def remote(src, dst, ssem, rsem, dp_to, ep_to):
        return pltpu.make_async_remote_copy(
            src_ref=src, dst_ref=dst, send_sem=ssem, recv_sem=rsem,
            device_id=(dp_to, ep_to), device_id_type=MESH)

    def peer(dz):
        zz = lax.rem(z + dz, N_Z)
        return zz, zz * 2 + c

    def other(i):
        return lax.rem(r + N_DP * N_DP + (1 - 2 * c) * i, N_DP)

    barrier = pltpu.get_barrier_semaphore()

    def greet(i, carry):
        pl.semaphore_signal(barrier, inc=1, device_id=(lax.rem(r + i, N_DP), ep), device_id_type=MESH)
        return carry

    lax.fori_loop(1, N_DP, greet, 0)
    pl.semaphore_signal(barrier, inc=1, device_id=(r, sib), device_id_type=MESH)
    for dz in (1, 2, 3):
        pl.semaphore_signal(barrier, inc=1, device_id=(r, peer(dz)[1]), device_id_type=MESH)

    loads = [
        (lat_h, lat), (kr_h, kr), (vu_h, vu), (op_h, op), (routes_h, rt.at[z]),
        (gain_h, gain), (router_h, router), (gu_h.at[0], gu), (dn_h.at[0], dn), (lengths_h, lengths_s), (plan_h, plan_s),
    ]
    load = [pltpu.make_async_copy(s, d, l_sem.at[i]) for i, (s, d) in enumerate(loads)]
    qload = []
    for b in range(8):
        to = (b % 2) * HALF + (b // 2) * SPAN
        qload.append(pltpu.make_async_copy(
            qc_h.at[pl.ds(b * SPAN, SPAN)], qc.at[pl.ds(to, SPAN)], q_sem.at[b]))
        qload.append(pltpu.make_async_copy(
            qr_h.at[pl.ds(b * SPAN, SPAN)], qr.at[pl.ds(to, SPAN)], q_sem.at[8 + b]))
    for i in (9, 10, 4):
        load[i].start()
    load[0].start()
    load[1].start()
    for cp in qload:
        cp.start()
    load[2].start()

    load[0].wait()
    load[1].wait()
    for cp in qload:
        cp.wait()
    for i in (3, 5, 6, 7, 8):
        load[i].start()
    load[9].wait()
    length = lengths_s[r]
    latv = lat[...]
    krv = kr[...]
    place = lax.broadcasted_iota(jnp.int32, (S, S), 0)
    position = ((place % HALF) // SPAN * 2 + place // HALF) * SPAN + place % SPAN
    load[2].wait()
    for h in range(HEADS_HERE):
        att = attend(
            qc[:, h * LAT:(h + 1) * LAT], qr[:, h * ROPE:(h + 1) * ROPE], latv, krv, position, length)
        vals[:, h * VDIM:(h + 1) * VDIM] = mm(att, vu[h]).astype(BF)

    pl.semaphore_wait(barrier, N_DP - 1 + 1 + 3)
    for dz in (1, 2, 3):
        pl.semaphore_signal(in_sem, inc=1, device_id=(r, peer(dz)[1]), device_id_type=MESH)

    load[4].wait()
    load[10].wait()

    def rt_copy(dz, slot):
        return remote(rt.at[slot], rt.at[slot], rt_s.at[dz], rt_r.at[slot], r, peer(dz)[1])

    for dz in (1, 2, 3):
        rt_copy(dz, z).start()

    load[3].wait()
    order = (2, 1, 3, 0)

    def px_copy(p, zz):
        return remote(px_send[p].at[zz], px_recv[p].at[zz], px_s.at[p, zz], px_r.at[p, zz], r, sib)

    def rs_copy(p, dz):
        zz, to = peer(dz)
        return remote(rs_send[p].at[zz], rs_recv[p].at[z], rs_s.at[p, dz], rs_r.at[p, z], r, to)

    def pair_sum(p, dz):
        zz, _ = peer(dz)
        px_copy(p, zz).wait_recv()
        total = own[p][zz] + px_recv[p][zz].astype(F32)
        if dz:
            rs_send[p][zz] = total.astype(BF)
            rs_copy(p, dz).start()
        else:
            own[p][zz] = total

    def ra_all():
        part = rt_all.at[pl.ds(0, N_DP - 1)]
        return remote(part, part, ra_s.at[0], ra_r.at[0], r, sib)

    def spread_routes():
        for dz in (1, 2, 3):
            rt_copy(dz, peer(dz)[0]).wait_recv()

        @pl.when(c == 1)
        def _():
            rt_all[r] = rt[N_Z - 1]

            def ra_start(i, carry):
                to = other(i)
                remote(rt_all.at[r], rt_all.at[r], ra_s.at[0], ra_r.at[0], to, ep).start()
                return carry

            lax.fori_loop(1, N_DP, ra_start, 0)

    valv = vals[...]
    steps = [(p, dz) for p in range(n_pieces) for dz in order]
    for n, (p, dz) in enumerate(steps):
        zz, _ = peer(dz)
        first, width = PIECES[p]
        block = mm(valv, op[:, pl.ds(pl.multiple_of(zz * COLS + first, 128), width)])
        top, bottom = block[:HALF], block[HALF:]
        own[p][zz] = jnp.where(c == 0, top, bottom)
        px_send[p][zz] = jnp.where(c == 0, bottom, top).astype(BF)
        px_copy(p, zz).start()
        if n >= LAG:
            pair_sum(*steps[n - LAG])
        if n == 4:
            spread_routes()
    for step in steps[len(steps) - LAG:]:
        pair_sum(*step)

    @pl.when(c == 1)
    def _():
        ra_all().wait_recv()
        rt_last[...] = rt_all[plan_s[r]]

    @pl.when(c == 0)
    def _():
        rt_last[...] = rt[N_Z - 1]

    slot = lax.broadcasted_iota(jnp.int32, (N_DP * SLOTS, HALF), 0)
    row = lax.broadcasted_iota(jnp.int32, (N_DP * SLOTS, HALF), 1)
    expert = slot // SLOTS
    t_row = lax.broadcasted_iota(jnp.int32, (HALF, HALF), 0)
    t_col = lax.broadcasted_iota(jnp.int32, (HALF, HALF), 1)
    earlier = jnp.where((t_row // SPAN == t_col // SPAN) & (t_row < t_col), 1.0, 0.0).astype(BF)
    same = (slot // 2) % N_Z == row // SPAN

    def slot_matrix(final):
        blocks = [rt[i] for i in range(N_Z - 1)] + [final]
        first = jnp.concatenate([block[0:1, :] for block in blocks], axis=1)
        second = jnp.concatenate([block[1:2, :] for block in blocks], axis=1)
        named = jnp.where((first == expert) | (second == expert), 1.0, 0.0)
        before = mm(named.astype(BF), earlier)
        return jnp.where(same & (before == (slot % 2).astype(F32)), named, 0.0)

    slots_t = slot_matrix(rt_last[...]).astype(BF)

    def a_copy(p, to, dz):
        return remote(
            a_send[p].at[to], x[p].at[z, c, r], a_s.at[p, dz], a_r.at[p, z], to, peer(dz)[1])

    for p, (first, width) in enumerate(PIECES):
        total = own[p][z]
        for dz in (1, 3, 2):
            zz, to = peer(dz)
            remote(rs_send[p].at[zz], rs_recv[p].at[zz], rs_s.at[p, dz], rs_r.at[p, zz], r, to).wait_recv()
            total = total + rs_recv[p][zz].astype(F32)
        a_send[p][...] = mm(slots_t, total.astype(BF)).reshape(N_DP, SLOTS, width).astype(BF)
        if p == 0:
            pl.semaphore_wait(in_sem, 3)

        def to_plane(planes):
            def a_start(i, carry):
                to = other(i)
                for dz in planes:
                    a_copy(p, to, dz).start()
                return carry

            lax.fori_loop(1, N_DP, a_start, 0)

        to_plane((0,))
        for dz in (1,):
            a_copy(p, r, dz).start()
        to_plane((1,))
        for dz in (3,):
            a_copy(p, r, dz).start()
        to_plane((3,))
        for dz in (2,):
            a_copy(p, r, dz).start()
        to_plane((2,))
        x[p][z, c, r] = a_send[p][r]

    slots = slot_matrix(rt[N_Z - 1]).T.astype(BF)

    half = N_DP * SLOTS
    to_row = lax.broadcasted_iota(jnp.int32, (2 * half, 2 * half), 0)
    from_row = lax.broadcasted_iota(jnp.int32, (2 * half, 2 * half), 1)
    rank = (to_row % half) // SLOTS
    partner = jnp.zeros_like(rank)
    for i in range(N_DP):
        partner = jnp.where(rank == i, plan_s[i], partner)
    moves = (to_row >= half) & (to_row % SLOTS >= SLOTS - 2)
    wanted = to_row + jnp.where(moves, (partner - rank) * SLOTS, 0)
    swap[...] = jnp.where(from_row == wanted, 1.0, 0.0).astype(BF)

    def a_wait(p, zz, count):
        part = x[p].at[zz, c, pl.ds(0, count)]
        remote(part, part, a_s.at[p, 0], a_r.at[p, zz], r, sib).wait_recv()

    def h_copy(p, zz, cc):
        return remote(x[p].at[zz, cc], x[p].at[zz, cc], h_s.at[p, zz], h_r.at[p, zz], r, sib)

    for i in (5, 6, 7, 8):
        load[i].wait()
    square[...] = jnp.zeros_like(square)
    gate[...] = jnp.zeros_like(gate)
    upper[...] = jnp.zeros_like(upper)
    logit[...] = jnp.zeros_like(logit)

    def expert_chunk(p, zz):
        first, width = PIECES[p]
        h_copy(p, zz, 1 - c).wait_recv()
        at = pl.multiple_of(zz * COLS + first, 128)
        m = x[p][zz].astype(F32).reshape(2 * half, width)
        square[...] += jnp.sum(m * m, axis=1, keepdims=True)
        xin = (m * gain[pl.ds(at, width)].reshape(1, width)).astype(BF)
        gate[...] += mm(xin, gu[0, pl.ds(at, width)])
        upper[...] += mm(xin, gu[1, pl.ds(at, width)])
        logit[...] += lax.dot_general(
            xin, router[:, pl.ds(at, width)], (((1,), (1,)), ((), ())), preferred_element_type=F32)

    previous = None
    for p in range(n_pieces):
        for dz in (0, 1, 3, 2):
            zz, _ = peer(dz)
            a_wait(p, zz, N_DP if dz else N_DP - 1)
            h_copy(p, zz, c).start()
            if previous is not None:
                expert_chunk(*previous)
            previous = (p, zz)
    expert_chunk(*previous)

    scale = lax.rsqrt(square[...] * (1.0 / D) + norm_eps)
    pick = lax.broadcasted_iota(jnp.int32, logit.shape, 1) == r
    chosen = jax.nn.sigmoid(jnp.sum(jnp.where(pick, logit[...], 0.0), axis=1, keepdims=True) * scale)
    swapv = swap[...]
    hidv = (jax.nn.silu(gate[...] * scale) * (upper[...] * scale) * chosen).astype(BF)
    hidv = mm(swapv, hidv).astype(BF)

    def ox_copy(p, zz):
        return remote(ox_send[p].at[zz], ox_recv[p].at[zz], ox_s.at[p, zz], ox_r.at[p, zz], r, sib)

    def c_copy(dz):
        zz, to = peer(dz)
        return remote(c_send.at[zz], c_recv.at[z], c_s.at[dz], c_r.at[z], r, to)

    def b_copy(zz, to):
        return remote(b_send.at[zz, to], b_recv.at[zz, r], b_s.at[zz], b_r.at[zz], to, ep)

    def b_all(zz):
        part = b_recv.at[zz, pl.ds(0, N_DP - 1)]
        return remote(part, part, b_s.at[zz], b_r.at[zz], r, sib)

    def d_copy(to):
        return remote(d_send.at[to], d_recv.at[r], d_s.at[0], d_r.at[0], to, ep)

    def d_all():
        part = d_recv.at[pl.ds(0, N_DP - 1)]
        return remote(part, part, d_s.at[0], d_r.at[0], r, sib)

    def to_ranks(make):
        def start(i, carry):
            make(other(i)).start()
            return carry

        lax.fori_loop(1, N_DP, start, 0)

    def out_sum(p, dz):
        zz, _ = peer(dz)
        first, width = BACK[p]
        ox_copy(p, zz).wait_recv()
        total = o_own[p][zz] + ox_recv[p][zz].astype(F32)
        if dz == 0:
            total = total + residual[:, first:first + width]
        if p == 1:
            b_send[zz] = total.reshape(N_DP, SLOTS, width).astype(BF)
            to_ranks(lambda to: b_copy(zz, to))
            b_recv[zz, r] = b_send[zz, r]
        elif dz:
            c_send[zz] = total.astype(BF)
            c_copy(dz).start()
        else:
            o_own[p][zz] = total

    for n, (p, dz) in enumerate(steps):
        zz, _ = peer(dz)
        first, width = BACK[p]
        block = mm(hidv, dn[:, pl.ds(pl.multiple_of(zz * COLS + first, 128), width)])
        top, bottom = block[:half], block[half:]
        ox_send[p][zz] = jnp.where(c == 0, bottom, top).astype(BF)
        ox_copy(p, zz).start()
        o_own[p][zz] = jnp.where(c == 0, top, bottom)
        if n == 3:
            column = lax.broadcasted_iota(jnp.int32, (2 * half, EXTRA), 1)
            high = chosen.astype(BF).astype(F32)
            tail = jnp.where(column == 0, high, jnp.where(column == 1, chosen - high, 0.0)).astype(BF)
            tail = mm(swapv, tail)
            chosen = tail[:, 0:1] + tail[:, 1:2]
            t_send[...] = jnp.where(c == 0, tail[:half], tail[half:]).reshape(N_DP, SLOTS, EXTRA).astype(BF)
            swap_half = jnp.where(c == 0, swapv[:half, :half], swapv[half:, half:])
            mine = jnp.where(c == 0, chosen[:half], chosen[half:]) * (1.0 / route_scale)
            for q, (start, size) in enumerate(PIECES):
                rows_in = x[q][z, c].astype(F32).reshape(half, size).astype(BF)
                residual[:, start:start + size] = mm(swap_half, rows_in) * mine
        if n >= 3:
            out_sum(*steps[n - 3])
    for step in steps[len(steps) - 3:]:
        out_sum(*step)

    total = o_own[0][z]
    for dz in (1, 3, 2):
        zz, to = peer(dz)
        remote(c_send.at[zz], c_recv.at[zz], c_s.at[dz], c_r.at[zz], r, to).wait_recv()
        total = total + c_recv[zz].astype(F32)
    d_send[...] = total.reshape(N_DP, SLOTS, BACK[0][1]).astype(BF)
    to_ranks(d_copy)
    d_recv[r] = d_send[r]

    def t_copy(to):
        return remote(t_send.at[to], t_recv.at[r], t_s.at[0], t_r.at[0], to, ep)

    to_ranks(t_copy)
    t_recv[r] = t_send[r]

    def f_copy(dz, zz):
        to_z, to = peer(dz)
        return remote(
            f_send.at[zz, to_z], f_recv.at[z, zz], f_s.at[zz, dz], f_r.at[z, zz], r, to)

    def e_copy(dz):
        to_z, to = peer(dz)
        return remote(e_send.at[to_z], e_recv.at[z], e_s.at[dz], e_r.at[z], r, to)

    for dz in order:
        zz, _ = peer(dz)
        b_all(zz).wait_recv()
        joined = mm(slots, b_recv[zz].astype(F32).reshape(half, BACK[1][1]).astype(BF))
        f_send[zz] = joined.reshape(N_Z, SPAN, BACK[1][1]).astype(BF)
        for to in (2, 1, 3):
            f_copy(to, zz).start()
    d_all().wait_recv()
    joined = mm(slots, d_recv[...].astype(F32).reshape(half, BACK[0][1]).astype(BF))
    e_send[...] = joined.reshape(N_Z, SPAN, BACK[0][1]).astype(BF)
    for dz in (2, 1, 3):
        e_copy(dz).start()
    e_recv[z] = e_send[z]
    t_part = t_recv.at[pl.ds(0, N_DP - 1)]
    remote(t_part, t_part, t_s.at[0], t_r.at[0], r, sib).wait_recv()
    weight[...] = mm(slots, t_recv[...].astype(F32).reshape(half, EXTRA).astype(BF)).reshape(
        N_Z, SPAN, EXTRA)
    mine = weight[z]
    factor = route_scale / (mine[:, 0:1] + mine[:, 1:2])

    def store(zz):
        columns = pl.ds(pl.multiple_of(zz * COLS, 128), COLS)
        return pltpu.make_async_copy(result.at[zz], out.at[:, columns], o_sem.at[zz])

    for dz in order:
        zz, _ = peer(dz)
        total = f_send[zz, z].astype(F32)
        for frm in (1, 3, 2):
            from_z, _ = peer(frm)
            remote(
                f_send.at[zz, z], f_recv.at[from_z, zz], f_s.at[zz, frm], f_r.at[from_z, zz], r, sib
            ).wait_recv()
            total = total + f_recv[from_z, zz].astype(F32)
        result[zz, :, BACK[1][0]:] = (total * factor).astype(BF)
    for dz in (0, 1, 3, 2):
        zz, to = peer(dz)
        if dz:
            remote(e_send.at[zz], e_recv.at[zz], e_s.at[dz], e_r.at[zz], r, to).wait_recv()
        result[zz, :, :BACK[1][0]] = (e_recv[zz].astype(F32) * factor).astype(BF)
        store(zz).start()

    for i in range(N_Z):
        store(i).wait()
    for dz in range(N_Z):
        zz, to = peer(dz)
        count = N_DP if dz else N_DP - 1
        b_all(zz).wait_send()
        for p in range(n_pieces):
            part = a_send[p].at[pl.ds(0, count)]
            remote(part, part, a_s.at[p, dz], a_r.at[p, zz], r, sib).wait_send()
            px_copy(p, zz).wait_send()
            ox_copy(p, zz).wait_send()
            h_copy(p, zz, c).wait_send()
            if dz:
                rs_copy(p, dz).wait_send()
        if dz:
            rt_copy(dz, z).wait_send()
            c_copy(dz).wait_send()
            e_copy(dz).wait_send()
            for chunk in range(N_Z):
                f_copy(dz, chunk).wait_send()
    remote(t_part, t_part, t_s.at[0], t_r.at[0], r, sib).wait_send()
    d_all().wait_send()

    @pl.when(c == 1)
    def _():
        ra_all().wait_send()


def per_device(
    queries_c, queries_r, latents, key_rope, value_up, out_proj, norm_gain, router, gate_up, down,
    routes, lengths, plan,
):
    any_spec = pl.BlockSpec(memory_space=pl.ANY)
    vm = pltpu.VMEM
    dma = pltpu.SemaphoreType.DMA
    half = N_DP * SLOTS
    scratch = [
        pltpu.SMEM((N_DP,), jnp.int32), pltpu.SMEM((N_DP,), jnp.int32),
        vm((S, HEADS_HERE * LAT), BF), vm((S, HEADS_HERE * ROPE), BF), vm((S, LAT), BF), vm((ROPE, S), BF),
        vm((HEADS_HERE, LAT, VDIM), BF), vm((HEADS_HERE * VDIM, D), BF), vm((D,), F32),
        vm((N_DP, D), BF), vm((2, D, 256), BF), vm((256, D), BF),
        vm((N_Z, 2, SPAN), jnp.int32), vm((N_DP, 2, SPAN), jnp.int32), vm((2, SPAN), jnp.int32),
        vm((S, HEADS_HERE * VDIM), BF),
        vm((2 * half, 256), F32), vm((2 * half, 256), F32), vm((2 * half, N_DP), F32), vm((2 * half, 1), F32),
        vm((2 * half, 2 * half), BF),
        vm((half, COLS), F32), vm((N_Z, half, BACK[0][1]), BF), vm((N_Z, half, BACK[0][1]), BF),
        vm((N_DP, SLOTS, BACK[0][1]), BF), vm((N_DP, SLOTS, BACK[0][1]), BF),
        vm((N_Z, SPAN, BACK[0][1]), BF), vm((N_Z, SPAN, BACK[0][1]), BF),
        vm((N_Z, N_DP, SLOTS, BACK[1][1]), BF), vm((N_Z, N_DP, SLOTS, BACK[1][1]), BF),
        vm((N_DP, SLOTS, EXTRA), BF), vm((N_DP, SLOTS, EXTRA), BF),
        vm((N_Z, N_Z, SPAN, BACK[1][1]), BF), vm((N_Z, N_Z, SPAN, BACK[1][1]), BF),
        vm((N_Z, SPAN, EXTRA), F32), vm((N_Z, SPAN, COLS), BF),
    ]
    widths = [width for _, width in PIECES]
    n_pieces = len(PIECES)
    scratch += [vm((N_Z, HALF, w), F32) for w in widths]
    for _ in range(4):
        scratch += [vm((N_Z, HALF, w), BF) for w in widths]
    scratch += [vm((N_DP, SLOTS, w), BF) for w in widths]
    scratch += [vm((N_Z, 2, N_DP, SLOTS, w), BF) for w in widths]
    backs = [width for _, width in BACK]
    scratch += [vm((N_Z, half, w), F32) for w in backs]
    for _ in range(2):
        scratch += [vm((N_Z, half, w), BF) for w in backs]
    by_piece = dma((n_pieces, 4))
    scratch += [
        dma((11,)), dma((16,)), dma((4,)), pltpu.SemaphoreType.REGULAR, dma((4,)), dma((4,)), dma((1,)), dma((1,)),
        by_piece, by_piece, by_piece, by_piece, by_piece, by_piece, by_piece, by_piece,
        by_piece, by_piece, dma((4,)), dma((4,)), dma((1,)), dma((1,)), dma((4, 4)), dma((4, 4)),
        dma((4,)), dma((4,)), dma((1,)), dma((1,)), dma((4,)), dma((4,)),
    ]
    return pl.pallas_call(
        kernel,
        out_shape=jax.ShapeDtypeStruct((SPAN, D), BF),
        in_specs=[any_spec] * 13,
        out_specs=any_spec,
        scratch_shapes=scratch,
        compiler_params=pltpu.CompilerParams(
            collective_id=0, has_side_effects=True, vmem_limit_bytes=56 * 1024 * 1024),
        cost_estimate=pl.CostEstimate(flops=3 * 10**9, bytes_accessed=16 * 10**6, transcendentals=10**6),
    )(
        lengths, plan, queries_c, queries_r, latents, key_rope, value_up, out_proj,
        norm_gain, router.T, gate_up, down, routes.T,
    )


def solution(mesh):
    placed = (
        P("dp", "ep"),
        P("dp", "ep"),
        P("dp", None),
        P(None, "dp"),
        P("ep", None, None),
        P("ep", None),
        P(),
        P(),
        P("dp", None, None, "ep"),
        P("dp", "ep", None),
        P(("dp", "ep"), None),
        P(),
        P(),
    )
    return jax.shard_map(
        per_device, mesh=mesh, in_specs=placed, out_specs=P(("dp", "ep"), None), check_vma=False
    )
```
